256 devices in a mesh: ens: 8 (over z), space: 32 (over y, x, core).
Axes of the slice: x: 4, y: 4, z: 8, core: 2. Of those that a mesh axis runs over, the one named last changes fastest.
Arguments:
- mesh_latent: bfloat16 [8, 2048, 1024], P('ens', 'space'), may hold values from -6 to 6
- grid_latent: bfloat16 [8192, 1024], P('space'), may hold values from -6 to 6
- edge_list: int32 [8192, 3], P('space'), may hold values from 0 to 2047, as said below
- target: float32 [8192, 100], P('space'), may hold values from -6 to 6
- cell_area: float32 [8192], P('space'), may hold values from 0.3 to 3
- var_weight: float32 [100], replicated, may hold values from 0.1 to 1
- w_query: bfloat16 [1024, 1024], replicated, may hold values from -0.1875 to 0.1875
- w_key: bfloat16 [1024, 1024], replicated, may hold values from -0.1875 to 0.1875
- w_value: bfloat16 [1024, 1024], replicated, may hold values from -0.1875 to 0.1875
- w_out_proj: bfloat16 [1024, 1024], replicated, may hold values from -0.1875 to 0.1875
- w_head: bfloat16 [1024, 100], replicated, may hold values from -0.1875 to 0.1875
Outputs:
- grad_query: float32 [1024, 1024], P('space')
- grad_key: float32 [1024, 1024], P('space')
- grad_value: float32 [1024, 1024], P('space')
- grad_proj: float32 [1024, 1024], P('space')
- grad_head: float32 [1024, 100], P('space')
The draws below stay inside these ranges and needn't reach their ends.
Inputs may be any that keep to these rules, and one draw needn't show every extreme that they name: `edge_list`: grid point g refers only to mesh nodes held by spatial block g // 256 or the blocks just before and after it, counted cyclically over the 32 blocks.
All inputs are finite; a program needn't handle non-finite values.
Results may differ from the reference program's by a relative error of at most 0.03.
Values may be sent and summed in bfloat16 or wider, within the bound.
A program may use at most 128 MiB of HBM per device.

```python
import math
import jax
import jax.numpy as jnp
from jax import lax

D = 1024
HEADS = 16
VAR = 100
KNN = 3
G_DEV = 256
M_DEV = 64
MEMBERS = 8
GRID = 8192
MESH = 2048


def draw_edge_list(key, part):
    key = jax.random.fold_in(key, 11)
    offset_key, node_key = jax.random.split(key)
    shard_count = MESH // M_DEV
    home_shard = jnp.arange(GRID, dtype=jnp.int32) // G_DEV
    offsets = jax.random.randint(offset_key, (GRID, KNN), -1, 2)
    node_pick = jax.random.randint(node_key, (GRID, KNN), 0, M_DEV)
    result = (home_shard[:, None] + offsets) % shard_count * M_DEV + node_pick
    result = result.at[0, 0].set(0).at[GRID - 1, 0].set(MESH - 1)
    return result.astype(jnp.int32)


def block_levels(stream_key, shape, pieces, low, top_value):
    gain = 1.0
    for position, shards_of in pieces:
        steps = jax.random.uniform(jax.random.fold_in(jax.random.fold_in(stream_key, 6), position), (shards_of,), jnp.float32, low / len(pieces), top_value / len(pieces))
        gain = gain * jnp.repeat(jnp.exp(steps), shape[position] // shards_of).reshape((-1,) + (1,) * (len(shape) - 1 - position))
    return gain


def gaussian(stream_key, extent, width, most, cuts=(), held_as=jnp.bfloat16):
    array = jax.random.normal(stream_key, extent, jnp.float32) * width
    if len(cuts) > 0:
        array = block_levels(stream_key, extent, cuts, -0.22, 0.18) * array
    return jnp.clip(array, min=-most, max=most).astype(held_as)


def setup_inputs(seed: int = 0) -> dict:
    keys = jax.random.split(jax.random.key(seed), 12)
    return {
        "mesh_latent": gaussian(keys[0], (MEMBERS, MESH, D), 1.0, 6.0, ((0, 8), (1, 32))),
        "grid_latent": gaussian(keys[1], (GRID, D), 1.0, 6.0, ((0, 32),)),
        "edge_list": draw_edge_list(jax.random.fold_in(keys[11], 71), 0),
        "target": gaussian(keys[3], (GRID, VAR), 1.0, 6.0, ((0, 32),), jnp.float32),
        "cell_area": jnp.clip(jnp.exp(math.log(3.0) - 2.3025851 * jax.random.uniform(keys[4], (GRID,), jnp.float32) ** block_levels(keys[4], (GRID,), ((0, 32),), -0.2, 0.2)), 0.3, 3.0),
        "var_weight": jnp.clip(jnp.exp(jax.random.uniform(keys[5], (VAR,), jnp.float32, math.log(0.1), math.log(1.0))), 0.1, 1.0),
        "w_query": gaussian(keys[6], (D, D), D ** -0.5, 0.1875),
        "w_key": gaussian(keys[7], (D, D), D ** -0.5, 0.1875),
        "w_value": gaussian(keys[8], (D, D), D ** -0.5, 0.1875),
        "w_out_proj": gaussian(keys[9], (D, D), D ** -0.5, 0.1875),
        "w_head": gaussian(keys[10], (D, VAR), D ** -0.5, 0.1875),
    }


FAIR_ALPHA = 0.95
SMOOTH_SQ = 0.0625

def smooth_slope(diff):
    return diff / jnp.sqrt(diff * diff + SMOOTH_SQ)

def forward_local(grid_rows, key_table, value_table, index_rows, w_query, w_out_proj, w_head):
    row_count, model_width = grid_rows.shape
    head_size = model_width // HEADS
    queries = jnp.dot(grid_rows, w_query, preferred_element_type=jnp.float32).astype(jnp.bfloat16).reshape(row_count, HEADS, head_size)
    key_rows = jnp.take(key_table, index_rows, axis=0).reshape(row_count, KNN, HEADS, head_size)
    value_rows = jnp.take(value_table, index_rows, axis=0).reshape(row_count, KNN, HEADS, head_size)
    scores = jnp.einsum('ghd,gkhd->ghk', queries.astype(jnp.float32), key_rows.astype(jnp.float32)) * head_size ** (-0.5)
    attention = jax.nn.softmax(scores, axis=-1)
    attention_low = attention.astype(jnp.bfloat16)
    attended = jnp.einsum('ghk,gkhd->ghd', attention_low.astype(jnp.float32), value_rows.astype(jnp.float32)).astype(jnp.bfloat16).reshape(row_count, model_width)
    hidden = (grid_rows.astype(jnp.float32) + jnp.dot(attended, w_out_proj, preferred_element_type=jnp.float32)).astype(jnp.bfloat16)
    prediction = jnp.dot(hidden, w_head, preferred_element_type=jnp.float32)
    return (prediction, (queries, key_rows, value_rows, attention, attention_low, attended, hidden))

def backward_local(saved_state, grad_pred, grid_rows, w_out_proj, w_head):
    queries, key_rows, value_rows, attention, attention_low, attended, hidden = saved_state
    row_count, model_width = grid_rows.shape
    head_size = model_width // HEADS
    grad_low = grad_pred.astype(jnp.bfloat16)
    grad_head = jnp.dot(hidden.T, grad_low, preferred_element_type=jnp.float32)
    grad_hidden = jnp.dot(grad_low, w_head.T, preferred_element_type=jnp.float32).astype(jnp.bfloat16)
    grad_proj = jnp.dot(attended.T, grad_hidden, preferred_element_type=jnp.float32)
    grad_att = jnp.dot(grad_hidden, w_out_proj.T, preferred_element_type=jnp.float32).astype(jnp.bfloat16).reshape(row_count, HEADS, head_size)
    grad_weight = jnp.einsum('ghd,gkhd->ghk', grad_att.astype(jnp.float32), value_rows.astype(jnp.float32))
    grad_values = jnp.einsum('ghk,ghd->gkhd', attention_low.astype(jnp.float32), grad_att.astype(jnp.float32)).astype(jnp.bfloat16).reshape(row_count * KNN, model_width)
    grad_scores = (attention * (grad_weight - lax.optimization_barrier(jnp.sum(attention * grad_weight, axis=-1, keepdims=True))) * head_size ** (-0.5)).astype(jnp.bfloat16)
    grad_queries = jnp.einsum('ghk,gkhd->ghd', grad_scores.astype(jnp.float32), key_rows.astype(jnp.float32)).astype(jnp.bfloat16).reshape(row_count, model_width)
    grad_keys = jnp.einsum('ghk,ghd->gkhd', grad_scores.astype(jnp.float32), queries.astype(jnp.float32)).astype(jnp.bfloat16).reshape(row_count * KNN, model_width)
    grad_query = jnp.dot(grid_rows.T, grad_queries, preferred_element_type=jnp.float32)
    return (grad_query, grad_proj, grad_head, grad_keys, grad_values)

def crps_grad(prediction, pair_sum, target_rows, area_rows, var_weight, members):
    fair_eps = (1.0 - FAIR_ALPHA) / members
    pair_coef = (1.0 - fair_eps) / (members * (members - 1))
    scaled = smooth_slope(prediction - target_rows) / members - pair_coef * pair_sum
    return area_rows[:, None] * var_weight[None, :] * scaled

def reference(mesh_latent, grid_latent, edge_list, target, cell_area, var_weight, w_query, w_key, w_value, w_out_proj, w_head):

    def member_pass(member):
        latent = mesh_latent[member]
        key_table = jnp.dot(latent, w_key, preferred_element_type=jnp.float32).astype(jnp.bfloat16)
        value_table = jnp.dot(latent, w_value, preferred_element_type=jnp.float32).astype(jnp.bfloat16)
        prediction, saved_state = forward_local(grid_latent, key_table, value_table, edge_list, w_query, w_out_proj, w_head)
        return (latent, prediction, saved_state)
    outputs = []
    for member in range(MEMBERS):
        outputs.append(member_pass(member)[1])
    ensemble = jnp.stack(outputs)
    flat_edges = edge_list.reshape(-1)
    model_width = grid_latent.shape[1]
    acc_query = jnp.zeros((model_width, model_width), jnp.float32)
    acc_key = jnp.zeros((model_width, model_width), jnp.float32)
    acc_value = jnp.zeros((model_width, model_width), jnp.float32)
    acc_proj = jnp.zeros((model_width, model_width), jnp.float32)
    acc_head = jnp.zeros((model_width, w_head.shape[1]), jnp.float32)
    for member in range(MEMBERS):
        latent, prediction, saved_state = member_pass(member)
        pair_sum = lax.optimization_barrier(jnp.sum(smooth_slope(prediction[None] - ensemble), axis=0))
        grad_pred = crps_grad(prediction, pair_sum, target, cell_area, var_weight, MEMBERS)
        grad_query, grad_proj, grad_head, grad_keys, grad_values = backward_local(saved_state, grad_pred, grid_latent, w_out_proj, w_head)
        gathered = jnp.take(latent, flat_edges, axis=0)
        acc_key = acc_key + jnp.dot(gathered.T, grad_keys, preferred_element_type=jnp.float32)
        acc_value = acc_value + jnp.dot(gathered.T, grad_values, preferred_element_type=jnp.float32)
        acc_query = acc_query + grad_query
        acc_proj = acc_proj + grad_proj
        acc_head = acc_head + grad_head
    return (acc_query, acc_key, acc_value, acc_proj, acc_head)
```

```python
import functools

import jax
import jax.numpy as jnp
from jax import lax
from jax.experimental import pallas as pl
from jax.experimental.pallas import tpu as pltpu
from jax.sharding import PartitionSpec as P

MESH = pl.DeviceIdType.MESH
HEADS = 16
KNN = 3
FAIR_ALPHA = 0.95
SMOOTH_SQ = 0.0625
ENS = 8
SPACE = 32
D = 1024
HD = D // HEADS
G = 256
M = 64
N = 3 * M
E = KNN * G
VAR = 100
VP = 128
C = D // ENS
ROWS = D // SPACE
W = 256
BF = jnp.bfloat16
F32 = jnp.float32


def dot(a, b):
    return jnp.dot(a, b, preferred_element_type=F32)


def slope(d):
    return d * lax.rsqrt(d * d + SMOOTH_SQ)


def same_head(width, value):
    rows = lax.broadcasted_iota(jnp.int32, (width, width), 0) // HD
    cols = lax.broadcasted_iota(jnp.int32, (width, width), 1) // HD
    return jnp.where(rows == cols, value, 0.0).astype(BF)


def softmax3(scores):
    s0, s1, s2 = scores[:G], scores[G : 2 * G], scores[2 * G :]
    top = jnp.maximum(jnp.maximum(s0, s1), s2)
    e0, e1, e2 = jnp.exp(s0 - top), jnp.exp(s1 - top), jnp.exp(s2 - top)
    inv = 1.0 / (e0 + e1 + e2)
    return e0 * inv, e1 * inv, e2 * inv


def main_kernel(
    x_ref, grid_ref, edge_ref, target_ref, area_ref, var_ref,
    wq_hbm, wk_hbm, wv_hbm, wo_hbm, wh_ref,
    out_ref,
    wq, wk, wv, wo, whp, lat, lat_t, grid_t, mix_t, q, keys, values, attended, hidden,
    delta, kvc, wkvc, kgv, att_all, gl, s_all, oh, oh_t, q3s, gq, uct, common, areaw,
    part_ab, part, r_ab, r, rz,
    wsem, ring_s, ring_r, halo_s, halo_l, halo_r, d_s, d_r, ab_s, ab_r, g_s, g_r, z_s, z_r,
):
    e = lax.axis_index("ens")
    s = lax.axis_index("space")

    loads = [
        pltpu.make_async_copy(src, dst, wsem.at[i])
        for i, (src, dst) in enumerate(((wq_hbm, wq), (wk_hbm, wk), (wv_hbm, wv), (wo_hbm, wo)))
    ]
    for load in loads:
        load.start()

    def ens_peer(d):
        return (lax.rem(e + d, ENS), s)

    def space_peer(d):
        return (e, lax.rem(s + d, SPACE))

    barrier = pltpu.get_barrier_semaphore()

    @pl.loop(1, ENS)
    def _(d):
        pl.semaphore_signal(barrier, inc=1, device_id=ens_peer(d), device_id_type=MESH)

    @pl.loop(1, SPACE)
    def _(d):
        pl.semaphore_signal(barrier, inc=1, device_id=space_peer(d), device_id_type=MESH)

    def own_rows(m):
        return pl.ds(pl.multiple_of(m * N + M, M), M)

    def low_rows(m):
        return pl.ds(pl.multiple_of(m * N, M), M)

    def high_rows(m):
        return pl.ds(pl.multiple_of(m * N + 2 * M, M), M)

    def member(d):
        return lax.rem(e + d + ENS, ENS)

    def ring_copy(m, step, way):
        return pltpu.make_async_remote_copy(
            src_ref=lat.at[own_rows(m)], dst_ref=lat.at[own_rows(m)],
            send_sem=ring_s.at[step], recv_sem=ring_r.at[m],
            device_id=ens_peer(way), device_id_type=MESH,
        )

    def halo_copies(m):
        up = pltpu.make_async_remote_copy(
            src_ref=lat.at[own_rows(m)], dst_ref=lat.at[low_rows(m)],
            send_sem=halo_s.at[m, 0], recv_sem=halo_l.at[m],
            device_id=space_peer(1), device_id_type=MESH,
        )
        down = pltpu.make_async_remote_copy(
            src_ref=lat.at[own_rows(m)], dst_ref=lat.at[high_rows(m)],
            send_sem=halo_s.at[m, 1], recv_sem=halo_r.at[m],
            device_id=space_peer(SPACE - 1), device_id_type=MESH,
        )
        return up, down

    def start_halo(m):
        up, down = halo_copies(m)
        up.start()
        down.start()

    lat[own_rows(e), :] = x_ref[...]
    whp[...] = jnp.zeros_like(whp)
    whp[:, :VAR] = wh_ref[...]
    loads[0].wait()

    @pl.loop(0, D // W)
    def _(n):
        cols = pl.ds(pl.multiple_of(n * W, W), W)
        q[:, cols] = dot(grid_ref[...], wq[:, cols]).astype(BF)

    pl.semaphore_wait(barrier, ENS - 1 + SPACE - 1)
    start_halo(e)
    forward = [ring_copy(member(-k + 1), k - 1, 1) for k in range(1, 5)]
    backward = [ring_copy(member(k - 1), 3 + k, ENS - 1) for k in range(1, 4)]
    forward[0].start()
    backward[0].start()

    def ring_arrived(m):
        ring_copy(m, 0, 1).wait_recv()
        start_halo(m)

    edges = edge_ref[...]
    slot_rows = (((edges // M) - s + 1 + SPACE) % SPACE) * M + edges % M
    node = lax.broadcasted_iota(jnp.int32, (G, N), 1)
    for j in range(KNN):
        oh[j * G : (j + 1) * G, :] = jnp.where(slot_rows[:, j : j + 1] == node, 1.0, 0.0).astype(BF)
    oh_t[...] = oh[...].T
    grid_t[...] = grid_ref[...].T
    var_row = jnp.concatenate([var_ref[...], jnp.zeros((1, VP - VAR), F32)], axis=1)
    areaw[...] = jnp.broadcast_to(area_ref[...], (VP, G)).T * var_row
    common[...] = dot(grid_ref[...], whp[...])
    loads[1].wait()
    loads[2].wait()
    loads[3].wait()
    hs = pl.ds(pl.multiple_of(e * C, C), C)
    wkvc[:, :C] = wk[:, hs]
    wkvc[:, C:] = wv[:, hs]
    uct[...] = dot(wo[hs, :], whp[...]).T.astype(BF)
    for j in range(KNN):
        q3s[j * G : (j + 1) * G, :] = q[:, hs]

    own_up, own_down = halo_copies(e)
    own_up.wait_recv()
    own_down.wait_recv()
    own_table = pl.ds(pl.multiple_of(e * N, M), N)

    @pl.loop(0, D // W)
    def _(n):
        cols = pl.ds(pl.multiple_of(n * W, W), W)
        keys[:, cols] = dot(lat[own_table, :], wk[:, cols]).astype(BF)
        values[:, cols] = dot(lat[own_table, :], wv[:, cols]).astype(BF)

    ring_arrived(member(-1))
    ring_arrived(member(1))
    forward[1].start()
    backward[1].start()

    @pl.loop(0, D // W)
    def _(n):
        cols = pl.ds(pl.multiple_of(n * W, W), W)
        key_rows = dot(oh[...], keys[:, cols]).astype(BF)
        qc = q[:, cols]
        prod = key_rows * jnp.concatenate([qc, qc, qc], axis=0)
        att = softmax3(dot(prod, same_head(W, HD**-0.5)))
        value_rows = dot(oh[...], values[:, cols])
        total = jnp.zeros((G, W), F32)
        for j in range(KNN):
            total += att[j].astype(BF).astype(F32) * value_rows[j * G : (j + 1) * G]
        attended[:, cols] = total.astype(BF)

    ring_arrived(member(-2))
    ring_arrived(member(2))
    forward[2].start()
    backward[2].start()

    @pl.loop(0, D // W)
    def _(n):
        cols = pl.ds(pl.multiple_of(n * W, W), W)
        update = dot(attended[...], wo[:, cols])
        hidden[:, cols] = (grid_ref[:, cols].astype(F32) + update).astype(BF)

    ring_arrived(member(-3))
    ring_arrived(member(3))
    forward[3].start()

    delta[e] = (dot(hidden[...], whp[...]) - common[...]).astype(BF)

    def delta_copy(d, m):
        return pltpu.make_async_remote_copy(
            src_ref=delta.at[e], dst_ref=delta.at[m],
            send_sem=d_s.at[d], recv_sem=d_r.at[m],
            device_id=ens_peer(d), device_id_type=MESH,
        )

    @pl.loop(1, ENS)
    def _(d):
        delta_copy(d, e).start()

    common[:, :VAR] = common[:, :VAR] - target_ref[...]
    mix_t[:D, :] = attended[...].T
    mix_t[D:, :] = hidden[...].T
    ring_arrived(member(-4))

    def halo_wait(m):
        up, down = halo_copies(m)
        up.wait_recv()
        down.wait_recv()

    @pl.loop(1, ENS)
    def _(d):
        halo_wait(lax.rem(e + d, ENS))

    @pl.loop(0, ENS)
    def _(m):
        table = pl.ds(pl.multiple_of(m * N, M), N)
        kvc[table, :] = dot(lat[table, :], wkvc[...]).astype(BF)
        rows = dot(oh[...], kvc[table, :]).astype(BF)
        kgv[m] = rows
        att = softmax3(dot(rows[:, :C] * q3s[...], same_head(C, HD**-0.5)))
        for j in range(KNN):
            att_all[m, j * G : (j + 1) * G, :] = att[j]

    @pl.loop(0, ENS // 2)
    def _(p):
        both = pl.ds(pl.multiple_of(p * 2 * N, 2 * N), 2 * N)
        lat_t[:, both] = lat[both, :].T

    @pl.loop(1, ENS)
    def _(d):
        delta_copy(d, lax.rem(e + d, ENS)).wait_recv()

    fair_eps = (1.0 - FAIR_ALPHA) / ENS
    pair_coef = (1.0 - fair_eps) / (ENS * (ENS - 1))
    step_rows = 16

    @pl.loop(0, G // step_rows)
    def _(i):
        rows = pl.ds(pl.multiple_of(i * step_rows, step_rows), step_rows)
        dev = [delta[m, rows, :].astype(F32) for m in range(ENS)]
        pair = [None] * ENS
        for a in range(ENS):
            for b in range(a + 1, ENS):
                t = slope(dev[a] - dev[b])
                pair[a] = t if pair[a] is None else pair[a] + t
                pair[b] = -t if pair[b] is None else pair[b] - t
        shift = common[rows, :]
        scale = areaw[rows, :]
        for m in range(ENS):
            grad = scale * (slope(dev[m] + shift) * (1.0 / ENS) - pair_coef * pair[m])
            gl[pl.ds(pl.multiple_of(m * G + i * step_rows, step_rows), step_rows), :] = grad.astype(BF)

    def reduce_copy(src, dst, sends, recvs, d):
        rows = pl.ds(pl.multiple_of(lax.rem(s + d, SPACE) * ROWS, ROWS), ROWS)
        return pltpu.make_async_remote_copy(
            src_ref=src.at[rows], dst_ref=dst.at[d], send_sem=sends.at[d], recv_sem=recvs.at[d],
            device_id=space_peer(d), device_id_type=MESH,
        )

    own_gl = pl.ds(pl.multiple_of(e * G, G), G)

    @pl.loop(0, 2 * D // W)
    def _(i):
        rows = pl.ds(pl.multiple_of(i * W, W), W)
        part = dot(mix_t[rows, :], gl[own_gl, :]).astype(BF)
        target_rows = pl.ds(pl.multiple_of(lax.rem(i, D // W) * W, W), W)
        target_cols = pl.ds(pl.multiple_of((i // (D // W)) * VP, VP), VP)
        part_ab[target_rows, target_cols] = part

    @pl.loop(1, SPACE)
    def _(d):
        reduce_copy(part_ab, r_ab, ab_s, ab_r, d).start()

    gq[...] = jnp.zeros_like(gq)

    @pl.loop(0, ENS)
    def _(m):
        gl_rows = pl.ds(pl.multiple_of(m * G, G), G)
        ga = dot(gl[gl_rows, :], uct[...]).astype(BF)
        ga3 = jnp.concatenate([ga, ga, ga], axis=0)
        gw = dot(kgv[m, :, C:] * ga3, same_head(C, 1.0))
        att = att_all[m]
        t = att * gw
        tot = t[:G] + t[G : 2 * G] + t[2 * G :]
        gs = att * (gw - jnp.concatenate([tot, tot, tot], axis=0)) * HD**-0.5
        gs_low = gs.astype(BF)
        gqe = gs_low.astype(F32) * kgv[m, :, :C].astype(F32)
        gq[...] += gqe[:G] + gqe[G : 2 * G] + gqe[2 * G :]
        edge_grads = jnp.concatenate([gs_low * q3s[...], att.astype(BF) * ga3], axis=1)
        table = pl.ds(pl.multiple_of(m * N, M), N)
        s_all[table, :] = dot(oh_t[...], edge_grads).astype(BF)

    part[:, :C] = dot(grid_t[...], gq[...].astype(BF)).astype(BF)

    @pl.loop(0, D // W)
    def _(i):
        rows = pl.ds(pl.multiple_of(i * W, W), W)
        part[rows, C:] = dot(lat_t[rows, :], s_all[...]).astype(BF)

    @pl.loop(1, SPACE)
    def _(d):
        reduce_copy(part, r, g_s, g_r, d).start()

    own_out = pl.ds(pl.multiple_of(s * ROWS, ROWS), ROWS)
    r_ab[0] = part_ab[own_out, :]
    r[0] = part[own_out, :]

    @pl.loop(1, SPACE)
    def _(d):
        reduce_copy(part_ab, r_ab, ab_s, ab_r, d).wait_recv()

    rz[e, :, 3 * C :] = jnp.sum(r_ab[...].astype(F32), axis=0).astype(BF)

    @pl.loop(1, SPACE)
    def _(d):
        reduce_copy(part, r, g_s, g_r, d).wait_recv()

    rz[e, :, : 3 * C] = jnp.sum(r[...].astype(F32), axis=0).astype(BF)

    def last_copy(d, m):
        return pltpu.make_async_remote_copy(
            src_ref=rz.at[e], dst_ref=rz.at[m], send_sem=z_s.at[d], recv_sem=z_r.at[m],
            device_id=ens_peer(d), device_id_type=MESH,
        )

    @pl.loop(1, ENS)
    def _(d):
        last_copy(d, e).start()

    for copy in forward + backward:
        copy.wait_send()

    @pl.loop(0, ENS)
    def _(m):
        up, down = halo_copies(m)
        up.wait_send()
        down.wait_send()

    @pl.loop(1, ENS)
    def _(d):
        delta_copy(d, e).wait_send()

    @pl.loop(1, SPACE)
    def _(d):
        reduce_copy(part_ab, r_ab, ab_s, ab_r, d).wait_send()
        reduce_copy(part, r, g_s, g_r, d).wait_send()

    @pl.loop(1, ENS)
    def _(d):
        last_copy(d, e).wait_send()
        last_copy(d, lax.rem(e + d, ENS)).wait_recv()

    out_ref[...] = rz[...]


def finish_kernel(rz_ref, wh_ref, q_ref, k_ref, v_ref, p_ref, h_ref):
    for m in range(ENS):
        cols = slice(m * C, (m + 1) * C)
        q_ref[:, cols] = rz_ref[m, :, :C].astype(F32)
        k_ref[:, cols] = rz_ref[m, :, C : 2 * C].astype(F32)
        v_ref[:, cols] = rz_ref[m, :, 2 * C : 3 * C].astype(F32)
    mixed = rz_ref[0, :, 3 * C :].astype(F32)
    for m in range(1, ENS):
        mixed += rz_ref[m, :, 3 * C :].astype(F32)
    h_ref[...] = mixed[:, VP : VP + VAR]
    p_ref[...] = lax.dot_general(
        mixed[:, :VAR].astype(BF), wh_ref[...], (((1,), (1,)), ((), ())), preferred_element_type=F32
    )


def local(x, grid, edges, target, area, var, wq, wk, wv, wo, wh):
    vmem = pl.BlockSpec(memory_space=pltpu.VMEM)
    anywhere = pl.BlockSpec(memory_space=pl.ANY)
    dma = pltpu.SemaphoreType.DMA
    scratch = [
        pltpu.VMEM((D, D), BF), pltpu.VMEM((D, D), BF), pltpu.VMEM((D, D), BF), pltpu.VMEM((D, D), BF),
        pltpu.VMEM((D, VP), BF),
        pltpu.VMEM((ENS * N, D), BF), pltpu.VMEM((D, ENS * N), BF),
        pltpu.VMEM((D, G), BF), pltpu.VMEM((2 * D, G), BF),
        pltpu.VMEM((G, D), BF), pltpu.VMEM((N, D), BF), pltpu.VMEM((N, D), BF),
        pltpu.VMEM((G, D), BF), pltpu.VMEM((G, D), BF),
        pltpu.VMEM((ENS, G, VP), BF),
        pltpu.VMEM((ENS * N, 2 * C), BF), pltpu.VMEM((D, 2 * C), BF),
        pltpu.VMEM((ENS, E, 2 * C), BF), pltpu.VMEM((ENS, E, C), F32),
        pltpu.VMEM((ENS * G, VP), BF), pltpu.VMEM((ENS * N, 2 * C), BF),
        pltpu.VMEM((E, N), BF), pltpu.VMEM((N, E), BF),
        pltpu.VMEM((E, C), BF), pltpu.VMEM((G, C), F32), pltpu.VMEM((VP, C), BF),
        pltpu.VMEM((G, VP), F32), pltpu.VMEM((G, VP), F32),
        pltpu.VMEM((D, 2 * VP), BF), pltpu.VMEM((D, 3 * C), BF),
        pltpu.VMEM((SPACE, ROWS, 2 * VP), BF), pltpu.VMEM((SPACE, ROWS, 3 * C), BF),
        pltpu.VMEM((ENS, ROWS, 3 * C + 2 * VP), BF),
        dma((4,)), dma((7,)), dma((ENS,)), dma((ENS, 2)), dma((ENS,)), dma((ENS,)),
        dma((ENS,)), dma((ENS,)), dma((SPACE,)), dma((SPACE,)), dma((SPACE,)), dma((SPACE,)),
        dma((ENS,)), dma((ENS,)),
    ]
    rz = pl.pallas_call(
        main_kernel,
        out_shape=jax.ShapeDtypeStruct((ENS, ROWS, 3 * C + 2 * VP), BF),
        in_specs=[vmem] * 6 + [anywhere] * 4 + [vmem],
        out_specs=vmem,
        scratch_shapes=scratch,
        compiler_params=pltpu.CompilerParams(
            collective_id=0, has_side_effects=True, vmem_limit_bytes=56 << 20
        ),
        name="ensemble_gradients",
    )(x[0], grid, edges, target, area.reshape(1, G), var.reshape(1, VAR), wq, wk, wv, wo, wh)
    full = jax.ShapeDtypeStruct((ROWS, D), F32)
    return pl.pallas_call(
        finish_kernel,
        out_shape=(full, full, full, full, jax.ShapeDtypeStruct((ROWS, VAR), F32)),
        in_specs=[vmem, vmem],
        out_specs=(vmem,) * 5,
        name="finish",
    )(rz, wh)


def solution(mesh):
    in_specs = (
        P("ens", "space", None),
        P("space", None),
        P("space", None),
        P("space", None),
        P("space"),
        P(),
        P(),
        P(),
        P(),
        P(),
        P(),
    )
    out_specs = (P("space", None),) * 5
    return jax.shard_map(local, mesh=mesh, in_specs=in_specs, out_specs=out_specs, check_vma=False)
```

```python
import functools

import jax
import jax.numpy as jnp
from jax import lax
from jax.experimental import pallas as pl
from jax.experimental.pallas import tpu as pltpu
from jax.sharding import PartitionSpec as P

MESH = pl.DeviceIdType.MESH
HEADS = 16
KNN = 3
FAIR_ALPHA = 0.95
SMOOTH_SQ = 0.0625
ENS = 8
SPACE = 32
CX = 4
CY = 4
CHIPS = CX * CY
D = 1024
HD = D // HEADS
G = 256
M = 64
N = 3 * M
E = KNN * G
VAR = 100
VP = 128
C = D // ENS
ROWS = D // SPACE
W = 256
PAIRS = ENS // 2
BF = jnp.bfloat16
F32 = jnp.float32


def dot(a, b):
    return jnp.dot(a, b, preferred_element_type=F32)


def dot_nt(a, b):
    return lax.dot_general(a, b, (((1,), (1,)), ((), ())), preferred_element_type=F32)


def slope(d):
    return d * lax.rsqrt(d * d + SMOOTH_SQ)


def same_head(width, value):
    rows = lax.broadcasted_iota(jnp.int32, (width, width), 0) // HD
    cols = lax.broadcasted_iota(jnp.int32, (width, width), 1) // HD
    return jnp.where(rows == cols, value, 0.0).astype(BF)


def softmax3(scores):
    s0, s1, s2 = scores[:G], scores[G : 2 * G], scores[2 * G :]
    top = jnp.maximum(jnp.maximum(s0, s1), s2)
    e0, e1, e2 = jnp.exp(s0 - top), jnp.exp(s1 - top), jnp.exp(s2 - top)
    inv = 1.0 / (e0 + e1 + e2)
    return e0 * inv, e1 * inv, e2 * inv


def three(x):
    return jnp.concatenate([x, x, x], axis=0)


def side(x, y):
    return jnp.concatenate([x, y], axis=1)


PLACE = {0: 0, -1: 1, 1: 2, -2: 3, 2: 4, -3: 5, 3: 6, -4: 7}


def main_kernel(
    x_ref, grid_ref, edge_ref, target_ref, area_ref, var_ref,
    wq_hbm, wk_hbm, wv_hbm, wo_hbm, wh_ref,
    out_ref,
    wq, wk, wv, wo, wht, lat, lat_t, grid_t, mix_t, q, keys, values, attended, hidden,
    delta, wkvc, kg, vg, att_all, att_low, gl, ga, s_v, s_k, oh, oh_t, q3, gq, uct, common, areaw,
    part_ab, part_v, part_qk, sib_ab, sib_v, sib_qk, sum_ab, sum_v, sum_qk, r_ab, r_v, r_qk, rz,
    wsem, ring_s, ring_r, halo_s, halo_l, halo_r, d_s, d_r, sib_s, sib_r, xy_s, xy_r, z_s, z_r,
):
    e = lax.axis_index("ens")
    s = lax.axis_index("space")
    core = lax.rem(s, 2)
    chip_x = lax.rem(s // 2, CX)
    chip_y = s // (2 * CX)

    loads = [
        pltpu.make_async_copy(src, dst, wsem.at[i])
        for i, (src, dst) in enumerate(((wq_hbm, wq), (wk_hbm, wk), (wv_hbm, wv), (wo_hbm, wo)))
    ]
    for load in loads:
        load.start()

    def ens_peer(d):
        return (lax.rem(e + d + ENS, ENS), s)

    def space_peer(d):
        return (e, lax.rem(s + d + SPACE, SPACE))

    def chip_peer(t):
        return lax.rem(chip_y + t // CX, CY) * CX + lax.rem(chip_x + lax.rem(t, CX), CX)

    sibling = (e, s + 1 - 2 * core)

    barrier = pltpu.get_barrier_semaphore()

    def greet(peer):
        pl.semaphore_signal(barrier, inc=1, device_id=peer, device_id_type=MESH)

    greet(space_peer(1))
    greet(space_peer(-1))

    @pl.loop(1, ENS)
    def _(d):
        greet(ens_peer(d))

    @pl.loop(1, CHIPS)
    def _(t):
        greet((e, chip_peer(t) * 2 + core))

    def own_rows(i):
        return pl.ds(i * N + M, M)

    def ring_copy(d_from, d_to, sem, way):
        return pltpu.make_async_remote_copy(
            src_ref=lat.at[own_rows(PLACE[d_from])], dst_ref=lat.at[own_rows(PLACE[d_to])],
            send_sem=ring_s.at[sem], recv_sem=ring_r.at[PLACE[d_to]],
            device_id=ens_peer(way), device_id_type=MESH,
        )

    forward = {k: ring_copy(1 - k, -k, k - 1, 1) for k in range(1, 5)}
    backward = {k: ring_copy(k - 1, k, 3 + k, -1) for k in range(1, 4)}

    def halo_copies(i):
        up = pltpu.make_async_remote_copy(
            src_ref=lat.at[own_rows(i)], dst_ref=lat.at[pl.ds(i * N, M)],
            send_sem=halo_s.at[i, 0], recv_sem=halo_l.at[i],
            device_id=space_peer(1), device_id_type=MESH,
        )
        down = pltpu.make_async_remote_copy(
            src_ref=lat.at[own_rows(i)], dst_ref=lat.at[pl.ds(i * N + 2 * M, M)],
            send_sem=halo_s.at[i, 1], recv_sem=halo_r.at[i],
            device_id=space_peer(-1), device_id_type=MESH,
        )
        return up, down

    def start_halo(i):
        for copy in halo_copies(i):
            copy.start()

    def wait_halo(i):
        for copy in halo_copies(i):
            copy.wait_recv()

    def arrived(copy, d):
        copy.wait_recv()
        start_halo(PLACE[d])

    lat[own_rows(0), :] = x_ref[...]
    wht[...] = jnp.zeros_like(wht)
    wht[:VAR, :] = wh_ref[...]
    loads[0].wait()
    for n in range(D // W):
        cols = slice(n * W, (n + 1) * W)
        q[:, cols] = dot(grid_ref[...], wq[:, cols]).astype(BF)

    pl.semaphore_wait(barrier, 2 + ENS - 1 + CHIPS - 1)
    start_halo(0)
    forward[1].start()
    backward[1].start()

    edges = edge_ref[...]
    slot_rows = (((edges // M) - s + 1 + SPACE) % SPACE) * M + edges % M
    node = lax.broadcasted_iota(jnp.int32, (N, G), 0)
    for j in range(KNN):
        oh_t[:, j * G : (j + 1) * G] = jnp.where(slot_rows[j : j + 1, :] == node, 1.0, 0.0).astype(BF)
    oh[...] = oh_t[...].T
    grid_t[...] = grid_ref[...].T
    var_row = jnp.concatenate([var_ref[...], jnp.zeros((1, VP - VAR), F32)], axis=1)
    areaw[...] = jnp.broadcast_to(area_ref[...], (VP, G)).T * var_row
    common[...] = dot_nt(grid_ref[...], wht[...])
    for load in loads[1:]:
        load.wait()
    hs = pl.ds(pl.multiple_of(e * C, C), C)
    wkvc[:, :C] = wk[:, hs]
    wkvc[:, C:] = wv[:, hs]
    uct[...] = dot_nt(wht[...], wo[hs, :]).astype(BF)
    q3[...] = three(side(q[:, hs], q[:, hs]))

    wait_halo(0)
    for n in range(D // W):
        cols = slice(n * W, (n + 1) * W)
        keys[:, cols] = dot(lat[:N, :], wk[:, cols]).astype(BF)
        values[:, cols] = dot(lat[:N, :], wv[:, cols]).astype(BF)

    arrived(forward[1], -1)
    arrived(backward[1], 1)
    forward[2].start()
    backward[2].start()

    head_sum = same_head(W, HD**-0.5)
    for n in range(D // W):
        cols = slice(n * W, (n + 1) * W)
        prod = dot(oh[...], keys[:, cols]).astype(BF) * three(q[:, cols])
        att = softmax3(dot(prod, head_sum))
        value_rows = dot(oh[...], values[:, cols])
        total = jnp.zeros((G, W), F32)
        for j in range(KNN):
            total += att[j].astype(BF).astype(F32) * value_rows[j * G : (j + 1) * G]
        attended[:, cols] = total.astype(BF)

    for n in range(D // W):
        cols = slice(n * W, (n + 1) * W)
        update = dot(attended[...], wo[:, cols])
        hidden[:, cols] = (grid_ref[:, cols].astype(F32) + update).astype(BF)

    delta[0] = (dot_nt(hidden[...], wht[...]) - common[...]).astype(BF)

    def delta_copy(d):
        place = PLACE[-d if d <= ENS // 2 else ENS - d]
        return pltpu.make_async_remote_copy(
            src_ref=delta.at[0], dst_ref=delta.at[place],
            send_sem=d_s.at[d], recv_sem=d_r.at[place],
            device_id=ens_peer(d), device_id_type=MESH,
        )

    for d in (4, 3, 5, 2, 6, 1, 7):
        delta_copy(d).start()

    def prepare(p):
        rows = slice(2 * p * N, 2 * (p + 1) * N)
        kv = dot(lat[rows, :], wkvc[...]).astype(BF)
        kg[p] = dot(oh[...], side(kv[:N, :C], kv[N:, :C])).astype(BF)
        vg[p] = dot(oh[...], side(kv[:N, C:], kv[N:, C:])).astype(BF)
        att = softmax3(dot(kg[p] * q3[...], head_sum))
        for j in range(KNN):
            att_all[p, j * G : (j + 1) * G, :] = att[j]
            att_low[p, j * G : (j + 1) * G, :] = att[j].astype(BF)
        lat_t[:, rows] = lat[rows, :].T

    arrived(forward[2], -2)
    arrived(backward[2], 2)
    forward[3].start()
    backward[3].start()
    wait_halo(1)
    prepare(0)
    padded = jnp.concatenate([target_ref[...], jnp.zeros((VP - VAR, G), F32)], axis=0)
    common[...] = common[...] - padded.T
    arrived(forward[3], -3)
    arrived(backward[3], 3)
    forward[4].start()
    wait_halo(2)
    wait_halo(3)
    prepare(1)
    mix_t[:D, :] = attended[...].T
    mix_t[D:, :] = hidden[...].T
    wait_halo(4)
    wait_halo(5)
    prepare(2)
    arrived(forward[4], -4)
    wait_halo(6)
    wait_halo(7)
    prepare(3)

    for d in range(1, ENS):
        delta_copy(d).wait_recv()

    fair_eps = (1.0 - FAIR_ALPHA) / ENS
    pair_coef = (1.0 - fair_eps) / (ENS * (ENS - 1))
    step_rows = 16

    @pl.loop(0, G // step_rows)
    def _(i):
        rows = pl.ds(pl.multiple_of(i * step_rows, step_rows), step_rows)
        dev = [delta[m, rows, :].astype(F32) for m in range(ENS)]
        pair = [None] * ENS
        for a in range(ENS):
            for b in range(a + 1, ENS):
                t = slope(dev[a] - dev[b])
                pair[a] = t if pair[a] is None else pair[a] + t
                pair[b] = -t if pair[b] is None else pair[b] - t
        shift = common[rows, :]
        scale = areaw[rows, :]
        for m in range(ENS):
            grad = scale * (slope(dev[m] + shift) * (1.0 / ENS) - pair_coef * pair[m])
            gl[pl.ds(pl.multiple_of(m * G + i * step_rows, step_rows), step_rows), :] = grad.astype(BF)

    def sibling_copy(i, part, sib):
        return pltpu.make_async_remote_copy(
            src_ref=part.at[1 - core], dst_ref=sib, send_sem=sib_s.at[i], recv_sem=sib_r.at[i],
            device_id=sibling, device_id_type=MESH,
        )

    def chip_copy(i, summed, r, t):
        chip = chip_peer(t)
        return pltpu.make_async_remote_copy(
            src_ref=summed.at[pl.ds(pl.multiple_of(chip * ROWS, ROWS), ROWS)], dst_ref=r.at[t],
            send_sem=xy_s.at[i, t], recv_sem=xy_r.at[i, t],
            device_id=(e, chip * 2 + core), device_id_type=MESH,
        )

    def spread(i, part, sib, summed, r):
        sibling_copy(i, part, sib).wait_recv()
        summed[...] = (part[core].astype(F32) + sib[...].astype(F32)).astype(BF)

        @pl.loop(1, CHIPS)
        def _(t):
            chip_copy(i, summed, r, t).start()

        r[0] = summed[pl.ds(pl.multiple_of((s // 2) * ROWS, ROWS), ROWS), :]

    def last_copy(i, cols, d, m):
        return pltpu.make_async_remote_copy(
            src_ref=rz.at[e, :, cols], dst_ref=rz.at[m, :, cols],
            send_sem=z_s.at[i, d], recv_sem=z_r.at[i, m],
            device_id=ens_peer(d), device_id_type=MESH,
        )

    def collect(i, summed, r, cols):
        @pl.loop(1, CHIPS)
        def _(t):
            chip_copy(i, summed, r, t).wait_recv()

        rz[e, :, cols] = jnp.sum(r[...].astype(F32), axis=0).astype(BF)

        @pl.loop(1, ENS)
        def _(d):
            last_copy(i, cols, d, e).start()

    def put(part, chunk, cols, value):
        value = value.astype(BF)
        for k in range(W // ROWS):
            dest = chunk * (W // ROWS) + k
            rows = slice((dest // 2) * ROWS, (dest // 2 + 1) * ROWS)
            part[dest % 2, rows, cols] = value[k * ROWS : (k + 1) * ROWS, :]

    ab, v, qk = (0, part_ab, sib_ab), (1, part_v, sib_v), (2, part_qk, sib_qk)
    for i in range(D // W):
        rows = slice(i * W, (i + 1) * W)
        put(part_ab, i, slice(0, VP), dot(mix_t[rows, :], gl[:G, :]))
        put(part_ab, i, slice(VP, 2 * VP), dot(mix_t[D + i * W : D + (i + 1) * W, :], gl[:G, :]))
    sibling_copy(*ab).start()

    @pl.loop(0, ENS // 2)
    def _(p):
        rows = pl.ds(pl.multiple_of(p * 2 * G, 2 * G), 2 * G)
        both = dot(gl[rows, :], uct[...]).astype(BF)
        both = side(both[:G], both[G:])
        ga[p] = both
        sums = dot(oh_t[...], att_low[p] * three(both)).astype(BF)
        s_v[pl.ds(pl.multiple_of(p * 2 * N, N), N), :] = sums[:, :C]
        s_v[pl.ds(pl.multiple_of(p * 2 * N + N, N), N), :] = sums[:, C:]

    for i in range(D // W):
        put(part_v, i, slice(0, C), dot(lat_t[i * W : (i + 1) * W, :], s_v[...]))
    sibling_copy(*v).start()
    spread(*ab, sum_ab, r_ab)

    gq[...] = jnp.zeros_like(gq)
    ones = same_head(W, 1.0)

    @pl.loop(0, ENS // 2)
    def _(p):
        gw = dot(vg[p] * three(ga[p]), ones)
        att = att_all[p]
        t = att * gw
        gs = (att * (gw - three(t[:G] + t[G : 2 * G] + t[2 * G :])) * HD**-0.5).astype(BF)
        gqe = gs.astype(F32) * kg[p].astype(F32)
        gqe = gqe[:G] + gqe[G : 2 * G] + gqe[2 * G :]
        gq[...] += gqe[:, :C] + gqe[:, C:]
        sums = dot(oh_t[...], gs * q3[...]).astype(BF)
        s_k[pl.ds(pl.multiple_of(p * 2 * N, N), N), :] = sums[:, :C]
        s_k[pl.ds(pl.multiple_of(p * 2 * N + N, N), N), :] = sums[:, C:]

    spread(*v, sum_v, r_v)
    for i in range(D // W):
        rows = slice(i * W, (i + 1) * W)
        put(part_qk, i, slice(0, C), dot(grid_t[rows, :], gq[...].astype(BF)))
        put(part_qk, i, slice(C, 2 * C), dot(lat_t[rows, :], s_k[...]))
    sibling_copy(*qk).start()
    qk_cols, v_cols, ab_cols = slice(0, 2 * C), slice(2 * C, 3 * C), slice(3 * C, 3 * C + 2 * VP)
    collect(0, sum_ab, r_ab, ab_cols)
    spread(*qk, sum_qk, r_qk)
    collect(1, sum_v, r_v, v_cols)
    collect(2, sum_qk, r_qk, qk_cols)

    for copy in [*forward.values(), *backward.values()]:
        copy.wait_send()
    for i in range(ENS):
        for copy in halo_copies(i):
            copy.wait_send()
    for d in range(1, ENS):
        delta_copy(d).wait_send()
    for i, summed, r, cols in ((0, sum_ab, r_ab, ab_cols), (1, sum_v, r_v, v_cols), (2, sum_qk, r_qk, qk_cols)):
        sibling_copy(*(ab, v, qk)[i]).wait_send()

        @pl.loop(1, CHIPS)
        def _(t, i=i, summed=summed, r=r):
            chip_copy(i, summed, r, t).wait_send()

        @pl.loop(1, ENS)
        def _(d, i=i, cols=cols):
            last_copy(i, cols, d, e).wait_send()
            last_copy(i, cols, d, lax.rem(e + d, ENS)).wait_recv()

    out_ref[...] = rz[...]


def finish_kernel(rz_ref, wh_ref, q_ref, k_ref, v_ref, p_ref, h_ref):
    for m in range(ENS):
        cols = slice(m * C, (m + 1) * C)
        q_ref[:, cols] = rz_ref[m, :, :C].astype(F32)
        k_ref[:, cols] = rz_ref[m, :, C : 2 * C].astype(F32)
        v_ref[:, cols] = rz_ref[m, :, 2 * C : 3 * C].astype(F32)
    mixed = rz_ref[0, :, 3 * C :].astype(F32)
    for m in range(1, ENS):
        mixed += rz_ref[m, :, 3 * C :].astype(F32)
    h_ref[...] = mixed[:, VP : VP + VAR]
    p_ref[...] = dot(mixed[:, :VAR].astype(BF), wh_ref[...])


def local(x, grid, edges, target, area, var, wq, wk, wv, wo, wh):
    vmem = pl.BlockSpec(memory_space=pltpu.VMEM)
    anywhere = pl.BlockSpec(memory_space=pl.ANY)
    dma = pltpu.SemaphoreType.DMA
    widths = (2 * VP, C, 2 * C)
    scratch = [
        *[pltpu.VMEM((D, D), BF)] * 4,
        pltpu.VMEM((VP, D), BF),
        pltpu.VMEM((ENS * N, D), BF), pltpu.VMEM((D, ENS * N), BF),
        pltpu.VMEM((D, G), BF), pltpu.VMEM((2 * D, G), BF),
        pltpu.VMEM((G, D), BF), pltpu.VMEM((N, D), BF), pltpu.VMEM((N, D), BF),
        pltpu.VMEM((G, D), BF), pltpu.VMEM((G, D), BF),
        pltpu.VMEM((ENS, G, VP), BF), pltpu.VMEM((D, 2 * C), BF),
        pltpu.VMEM((PAIRS, E, W), BF), pltpu.VMEM((PAIRS, E, W), BF),
        pltpu.VMEM((PAIRS, E, W), F32), pltpu.VMEM((PAIRS, E, W), BF),
        pltpu.VMEM((ENS * G, VP), BF), pltpu.VMEM((PAIRS, G, W), BF),
        pltpu.VMEM((ENS * N, C), BF), pltpu.VMEM((ENS * N, C), BF),
        pltpu.VMEM((E, N), BF), pltpu.VMEM((N, E), BF),
        pltpu.VMEM((E, W), BF), pltpu.VMEM((G, C), F32), pltpu.VMEM((VP, C), BF),
        pltpu.VMEM((G, VP), F32), pltpu.VMEM((G, VP), F32),
        *[pltpu.VMEM((2, D // 2, w), BF) for w in widths],
        *[pltpu.VMEM((D // 2, w), BF) for w in widths],
        *[pltpu.VMEM((D // 2, w), BF) for w in widths],
        *[pltpu.VMEM((CHIPS, ROWS, w), BF) for w in widths],
        pltpu.VMEM((ENS, ROWS, 3 * C + 2 * VP), BF),
        dma((4,)), dma((7,)), dma((ENS,)), dma((ENS, 2)), dma((ENS,)), dma((ENS,)),
        dma((ENS,)), dma((ENS,)), dma((3,)), dma((3,)), dma((3, CHIPS)), dma((3, CHIPS)),
        dma((3, ENS)), dma((3, ENS)),
    ]
    rz = pl.pallas_call(
        main_kernel,
        out_shape=jax.ShapeDtypeStruct((ENS, ROWS, 3 * C + 2 * VP), BF),
        in_specs=[vmem] * 6 + [anywhere] * 4 + [vmem],
        out_specs=vmem,
        scratch_shapes=scratch,
        compiler_params=pltpu.CompilerParams(
            collective_id=0, has_side_effects=True, vmem_limit_bytes=56 << 20
        ),
        name="ensemble_gradients",
    )(x[0], grid, edges.T, target.T, area.reshape(1, G), var.reshape(1, VAR), wq, wk, wv, wo, wh.T)
    full = jax.ShapeDtypeStruct((ROWS, D), F32)
    return pl.pallas_call(
        finish_kernel,
        out_shape=(full, full, full, full, jax.ShapeDtypeStruct((ROWS, VAR), F32)),
        in_specs=[vmem, vmem],
        out_specs=(vmem,) * 5,
        name="finish",
    )(rz, wh.T)


def solution(mesh):
    in_specs = (
        P("ens", "space", None),
        P("space", None),
        P("space", None),
        P("space", None),
        P("space"),
        P(),
        P(),
        P(),
        P(),
        P(),
        P(),
    )
    out_specs = (P("space", None),) * 5
    return jax.shard_map(local, mesh=mesh, in_specs=in_specs, out_specs=out_specs, check_vma=False)
```

```python
import functools

import jax
import jax.numpy as jnp
from jax import lax
from jax.experimental import pallas as pl
from jax.experimental.pallas import tpu as pltpu
from jax.sharding import PartitionSpec as P

MESH = pl.DeviceIdType.MESH
HEADS = 16
KNN = 3
FAIR_ALPHA = 0.95
SMOOTH_SQ = 0.0625
ENS = 8
SPACE = 32
CX = 4
CY = 4
CHIPS = CX * CY
D = 1024
HD = D // HEADS
G = 256
M = 64
N = 3 * M
E = KNN * G
VAR = 100
VP = 128
C = D // ENS
ROWS = D // SPACE
W = 256
PAIRS = ENS // 2
BF = jnp.bfloat16
F32 = jnp.float32


def dot(a, b):
    return jnp.dot(a, b, preferred_element_type=F32)


def dot_nt(a, b):
    return lax.dot_general(a, b, (((1,), (1,)), ((), ())), preferred_element_type=F32)


def slope(d):
    return d * lax.rsqrt(d * d + SMOOTH_SQ)


def same_head(width, value):
    rows = lax.broadcasted_iota(jnp.int32, (width, width), 0) // HD
    cols = lax.broadcasted_iota(jnp.int32, (width, width), 1) // HD
    return jnp.where(rows == cols, value, 0.0).astype(BF)


def softmax3(scores):
    s0, s1, s2 = scores[:G], scores[G : 2 * G], scores[2 * G :]
    top = jnp.maximum(jnp.maximum(s0, s1), s2)
    e0, e1, e2 = jnp.exp(s0 - top), jnp.exp(s1 - top), jnp.exp(s2 - top)
    inv = 1.0 / (e0 + e1 + e2)
    return e0 * inv, e1 * inv, e2 * inv


def three(x):
    return jnp.concatenate([x, x, x], axis=0)


def side(x, y):
    return jnp.concatenate([x, y], axis=1)


PLACE = {0: 0, -1: 1, 1: 2, -2: 3, 2: 4, -3: 5, 3: 6, -4: 7, 4: 7}


def main_kernel(
    x_hbm, grid_hbm, edge_ref, target_hbm, area_ref, var_ref,
    wq_hbm, wk_hbm, wv_hbm, wo_hbm, wh_hbm,
    out_hbm,
    grid_ref, target_ref, wh_ref, wq, wk, wv, wo, wht, lat, lat_t, grid_t, mix_t, q, keys, values, attended, hidden,
    delta, wkvc, kg, vg, att_all, att_low, gl, ga, s_v, s_k, oh, oh_t, q3, gq, uct, common, areaw,
    part_ab, part_v, part_qk, sib_ab, sib_v, sib_qk, sum_ab, sum_v, sum_qk, r_ab, r_v, r_qk, rz,
    wsem, ring_s, ring_r, halo_s, halo_l, halo_r, d_s, d_r, sib_s, sib_r, xy_s, xy_r, z_s, z_r,
):
    e = lax.axis_index("ens")
    s = lax.axis_index("space")
    core = lax.rem(s, 2)
    chip_x = lax.rem(s // 2, CX)
    chip_y = s // (2 * CX)

    def ens_peer(d):
        return (lax.rem(e + d + ENS, ENS), s)

    def space_peer(d):
        return (e, lax.rem(s + d + SPACE, SPACE))

    def chip_peer(t):
        return lax.rem(chip_y + t // CX, CY) * CX + lax.rem(chip_x + lax.rem(t, CX), CX)

    sibling = (e, s + 1 - 2 * core)

    barrier = pltpu.get_barrier_semaphore()

    def greet(peer):
        pl.semaphore_signal(barrier, inc=1, device_id=peer, device_id_type=MESH)

    greet(space_peer(1))
    greet(space_peer(-1))

    @pl.loop(1, ENS)
    def _(d):
        greet(ens_peer(d))

    @pl.loop(1, CHIPS)
    def _(t):
        greet((e, chip_peer(t) * 2 + core))

    def own_rows(i):
        return pl.ds(i * N + M, M)

    def load(i, src, dst):
        copy = pltpu.make_async_copy(src, dst, wsem.at[i])
        copy.start()
        return copy

    load_x = load(0, x_hbm, lat.at[own_rows(0)])
    load_grid = load(1, grid_hbm, grid_ref)
    load_wq = load(2, wq_hbm, wq)
    loads = [
        load(i + 3, src, dst)
        for i, (src, dst) in enumerate(
            ((wh_hbm, wh_ref), (wk_hbm, wk), (wv_hbm, wv), (wo_hbm, wo), (target_hbm, target_ref))
        )
    ]

    def ring_copy(d_from, d_to, sem, way):
        src, dst = own_rows(PLACE[d_from]), own_rows(PLACE[d_to])
        if abs(d_to) == ENS // 2:
            half = 0 if way > 0 else M // 2
            src = pl.ds(PLACE[d_from] * N + M + half, M // 2)
            dst = pl.ds(PLACE[-4] * N + M + half, M // 2)
        return pltpu.make_async_remote_copy(
            src_ref=lat.at[src], dst_ref=lat.at[dst], send_sem=ring_s.at[sem], recv_sem=ring_r.at[sem],
            device_id=ens_peer(way), device_id_type=MESH,
        )

    forward = {k: ring_copy(1 - k, -k, k - 1, 1) for k in range(1, 5)}
    backward = {k: ring_copy(k - 1, k, 3 + k, -1) for k in range(1, 5)}

    def halo_copies(i):
        up = pltpu.make_async_remote_copy(
            src_ref=lat.at[own_rows(i)], dst_ref=lat.at[pl.ds(i * N, M)],
            send_sem=halo_s.at[i, 0], recv_sem=halo_l.at[i],
            device_id=space_peer(1), device_id_type=MESH,
        )
        down = pltpu.make_async_remote_copy(
            src_ref=lat.at[own_rows(i)], dst_ref=lat.at[pl.ds(i * N + 2 * M, M)],
            send_sem=halo_s.at[i, 1], recv_sem=halo_r.at[i],
            device_id=space_peer(-1), device_id_type=MESH,
        )
        return up, down

    def start_halo(i):
        for copy in halo_copies(i):
            copy.start()

    def wait_halo(i):
        for copy in halo_copies(i):
            copy.wait_recv()

    def arrived(copy, d):
        copy.wait_recv()
        start_halo(PLACE[d])

    load_grid.wait()
    load_wq.wait()
    for n in range(D // W):
        cols = slice(n * W, (n + 1) * W)
        q[:, cols] = dot(grid_ref[...], wq[:, cols]).astype(BF)

    load_x.wait()
    pl.semaphore_wait(barrier, 2 + ENS - 1 + CHIPS - 1)
    start_halo(0)
    forward[1].start()
    backward[1].start()

    for copy in loads:
        copy.wait()
    wht[...] = jnp.zeros_like(wht)
    wht[:VAR, :] = wh_ref[...]
    edges = edge_ref[...]
    slot_rows = (((edges // M) - s + 1 + SPACE) % SPACE) * M + edges % M
    node = lax.broadcasted_iota(jnp.int32, (N, G), 0)
    for j in range(KNN):
        oh_t[:, j * G : (j + 1) * G] = jnp.where(slot_rows[j : j + 1, :] == node, 1.0, 0.0).astype(BF)
    oh[...] = oh_t[...].T
    grid_t[...] = grid_ref[...].T
    var_row = jnp.concatenate([var_ref[...], jnp.zeros((1, VP - VAR), F32)], axis=1)
    areaw[...] = jnp.broadcast_to(area_ref[...], (VP, G)).T * var_row
    common[...] = dot_nt(grid_ref[...], wht[...])
    hs = pl.ds(pl.multiple_of(e * C, C), C)
    wkvc[:, :C] = wk[:, hs]
    wkvc[:, C:] = wv[:, hs]
    uct[...] = dot_nt(wht[...], wo[hs, :]).astype(BF)
    q3[...] = three(side(q[:, hs], q[:, hs]))

    wait_halo(0)
    for n in range(D // W):
        cols = slice(n * W, (n + 1) * W)
        keys[:, cols] = dot(lat[:N, :], wk[:, cols]).astype(BF)
        values[:, cols] = dot(lat[:N, :], wv[:, cols]).astype(BF)

    arrived(forward[1], -1)
    arrived(backward[1], 1)
    forward[2].start()
    backward[2].start()

    head_sum = same_head(W, HD**-0.5)
    for n in range(D // W):
        cols = slice(n * W, (n + 1) * W)
        prod = dot(oh[...], keys[:, cols]).astype(BF) * three(q[:, cols])
        att = softmax3(dot(prod, head_sum))
        value_rows = dot(oh[...], values[:, cols])
        total = jnp.zeros((G, W), F32)
        for j in range(KNN):
            total += att[j].astype(BF).astype(F32) * value_rows[j * G : (j + 1) * G]
        attended[:, cols] = total.astype(BF)

    for n in range(D // W):
        cols = slice(n * W, (n + 1) * W)
        update = dot(attended[...], wo[:, cols])
        hidden[:, cols] = (grid_ref[:, cols].astype(F32) + update).astype(BF)

    delta[0] = (dot_nt(hidden[...], wht[...]) - common[...]).astype(BF)

    def delta_copy(sem, d_from, d_to, way, rows=slice(None)):
        return pltpu.make_async_remote_copy(
            src_ref=delta.at[PLACE[d_from], rows], dst_ref=delta.at[PLACE[d_to], rows],
            send_sem=d_s.at[sem], recv_sem=d_r.at[sem],
            device_id=ens_peer(way), device_id_type=MESH,
        )

    near = [delta_copy(0, 0, -2, 2), delta_copy(1, 0, 2, -2), delta_copy(2, 0, -1, 1), delta_copy(3, 0, 1, -1)]
    far = [
        delta_copy(4, -2, -4, 2, pl.ds(0, G // 2)), delta_copy(5, 2, -4, -2, pl.ds(G // 2, G // 2)),
        delta_copy(6, -2, -3, 1), delta_copy(7, 2, 3, -1),
    ]
    for copy in near:
        copy.start()

    def prepare(p):
        rows = slice(2 * p * N, 2 * (p + 1) * N)
        kv = dot(lat[rows, :], wkvc[...]).astype(BF)
        kg[p] = dot(oh[...], side(kv[:N, :C], kv[N:, :C])).astype(BF)
        vg[p] = dot(oh[...], side(kv[:N, C:], kv[N:, C:])).astype(BF)
        att = softmax3(dot(kg[p] * q3[...], head_sum))
        for j in range(KNN):
            att_all[p, j * G : (j + 1) * G, :] = att[j]
            att_low[p, j * G : (j + 1) * G, :] = att[j].astype(BF)
        lat_t[:, rows] = lat[rows, :].T

    arrived(forward[2], -2)
    arrived(backward[2], 2)
    forward[3].start()
    backward[3].start()
    wait_halo(1)
    prepare(0)
    near[0].wait_recv()
    near[1].wait_recv()
    for copy in far:
        copy.start()
    padded = jnp.concatenate([target_ref[...], jnp.zeros((VP - VAR, G), F32)], axis=0)
    common[...] = common[...] - padded.T
    arrived(forward[3], -3)
    arrived(backward[3], 3)
    forward[4].start()
    backward[4].start()
    wait_halo(2)
    wait_halo(3)
    prepare(1)
    mix_t[:D, :] = attended[...].T
    mix_t[D:, :] = hidden[...].T
    wait_halo(4)
    wait_halo(5)
    prepare(2)
    backward[4].wait_recv()
    arrived(forward[4], -4)
    wait_halo(6)
    wait_halo(7)
    prepare(3)

    for copy in [*near[2:], *far]:
        copy.wait_recv()

    fair_eps = (1.0 - FAIR_ALPHA) / ENS
    pair_coef = (1.0 - fair_eps) / (ENS * (ENS - 1))
    step_rows = 16

    @pl.loop(0, G // step_rows)
    def _(i):
        rows = pl.ds(pl.multiple_of(i * step_rows, step_rows), step_rows)
        dev = [delta[m, rows, :].astype(F32) for m in range(ENS)]
        pair = [None] * ENS
        for a in range(ENS):
            for b in range(a + 1, ENS):
                t = slope(dev[a] - dev[b])
                pair[a] = t if pair[a] is None else pair[a] + t
                pair[b] = -t if pair[b] is None else pair[b] - t
        shift = common[rows, :]
        scale = areaw[rows, :]
        for m in range(ENS):
            grad = scale * (slope(dev[m] + shift) * (1.0 / ENS) - pair_coef * pair[m])
            gl[pl.ds(pl.multiple_of(m * G + i * step_rows, step_rows), step_rows), :] = grad.astype(BF)

    def sibling_copy(i, part, sib):
        return pltpu.make_async_remote_copy(
            src_ref=part.at[1 - core], dst_ref=sib, send_sem=sib_s.at[i], recv_sem=sib_r.at[i],
            device_id=sibling, device_id_type=MESH,
        )

    def chip_copy(i, summed, r, t):
        chip = chip_peer(t)
        return pltpu.make_async_remote_copy(
            src_ref=summed.at[pl.ds(pl.multiple_of(chip * ROWS, ROWS), ROWS)], dst_ref=r.at[t],
            send_sem=xy_s.at[i, t], recv_sem=xy_r.at[i, t],
            device_id=(e, chip * 2 + core), device_id_type=MESH,
        )

    def spread(i, part, sib, summed, r):
        sibling_copy(i, part, sib).wait_recv()
        summed[...] = (part[core].astype(F32) + sib[...].astype(F32)).astype(BF)

        @pl.loop(1, CHIPS)
        def _(t):
            chip_copy(i, summed, r, t).start()

        r[0] = summed[pl.ds(pl.multiple_of((s // 2) * ROWS, ROWS), ROWS), :]

    def last_copy(i, cols, d, m):
        return pltpu.make_async_remote_copy(
            src_ref=rz.at[e, :, cols], dst_ref=rz.at[m, :, cols],
            send_sem=z_s.at[i, d], recv_sem=z_r.at[i, m],
            device_id=ens_peer(d), device_id_type=MESH,
        )

    def collect(i, summed, r, cols):
        @pl.loop(1, CHIPS)
        def _(t):
            chip_copy(i, summed, r, t).wait_recv()

        rz[e, :, cols] = jnp.sum(r[...].astype(F32), axis=0).astype(BF)

        @pl.loop(1, ENS)
        def _(d):
            last_copy(i, cols, d, e).start()

    def put(part, chunk, cols, value):
        value = value.astype(BF)
        for k in range(W // ROWS):
            dest = chunk * (W // ROWS) + k
            rows = slice((dest // 2) * ROWS, (dest // 2 + 1) * ROWS)
            part[dest % 2, rows, cols] = value[k * ROWS : (k + 1) * ROWS, :]

    ab, v, qk = (0, part_ab, sib_ab), (1, part_v, sib_v), (2, part_qk, sib_qk)
    for i in range(D // W):
        rows = slice(i * W, (i + 1) * W)
        put(part_ab, i, slice(0, VP), dot(mix_t[rows, :], gl[:G, :]))
        put(part_ab, i, slice(VP, 2 * VP), dot(mix_t[D + i * W : D + (i + 1) * W, :], gl[:G, :]))
    sibling_copy(*ab).start()

    @pl.loop(0, ENS // 2)
    def _(p):
        rows = pl.ds(pl.multiple_of(p * 2 * G, 2 * G), 2 * G)
        both = dot(gl[rows, :], uct[...]).astype(BF)
        both = side(both[:G], both[G:])
        ga[p] = both
        sums = dot(oh_t[...], att_low[p] * three(both)).astype(BF)
        s_v[pl.ds(pl.multiple_of(p * 2 * N, N), N), :] = sums[:, :C]
        s_v[pl.ds(pl.multiple_of(p * 2 * N + N, N), N), :] = sums[:, C:]

    for i in range(D // W):
        put(part_v, i, slice(0, C), dot(lat_t[i * W : (i + 1) * W, :], s_v[...]))
    sibling_copy(*v).start()
    spread(*ab, sum_ab, r_ab)

    gq[...] = jnp.zeros_like(gq)
    ones = same_head(W, 1.0)

    @pl.loop(0, ENS // 2)
    def _(p):
        gw = dot(vg[p] * three(ga[p]), ones)
        att = att_all[p]
        t = att * gw
        gs = (att * (gw - three(t[:G] + t[G : 2 * G] + t[2 * G :])) * HD**-0.5).astype(BF)
        gqe = gs.astype(F32) * kg[p].astype(F32)
        gqe = gqe[:G] + gqe[G : 2 * G] + gqe[2 * G :]
        gq[...] += gqe[:, :C] + gqe[:, C:]
        sums = dot(oh_t[...], gs * q3[...]).astype(BF)
        s_k[pl.ds(pl.multiple_of(p * 2 * N, N), N), :] = sums[:, :C]
        s_k[pl.ds(pl.multiple_of(p * 2 * N + N, N), N), :] = sums[:, C:]

    spread(*v, sum_v, r_v)
    for i in range(D // W):
        rows = slice(i * W, (i + 1) * W)
        put(part_qk, i, slice(0, C), dot(grid_t[rows, :], gq[...].astype(BF)))
        put(part_qk, i, slice(C, 2 * C), dot(lat_t[rows, :], s_k[...]))
    sibling_copy(*qk).start()
    qk_cols, v_cols, ab_cols = slice(0, 2 * C), slice(2 * C, 3 * C), slice(3 * C, 3 * C + 2 * VP)
    spread(*qk, sum_qk, r_qk)
    collect(0, sum_ab, r_ab, ab_cols)
    collect(1, sum_v, r_v, v_cols)
    collect(2, sum_qk, r_qk, qk_cols)

    for copy in [*forward.values(), *backward.values(), *near, *far]:
        copy.wait_send()
    for i in range(ENS):
        for copy in halo_copies(i):
            copy.wait_send()
    stores = []
    for i, summed, r, cols in ((0, sum_ab, r_ab, ab_cols), (1, sum_v, r_v, v_cols), (2, sum_qk, r_qk, qk_cols)):
        sibling_copy(*(ab, v, qk)[i]).wait_send()

        @pl.loop(1, CHIPS)
        def _(t, i=i, summed=summed, r=r):
            chip_copy(i, summed, r, t).wait_send()

        @pl.loop(1, ENS)
        def _(d, i=i, cols=cols):
            last_copy(i, cols, d, e).wait_send()
            last_copy(i, cols, d, lax.rem(e + d, ENS)).wait_recv()

        stores.append(pltpu.make_async_copy(rz.at[:, :, cols], out_hbm.at[:, :, cols], wsem.at[i]))
        stores[-1].start()
    for store in stores:
        store.wait()


def finish_kernel(rz_ref, wh_ref, q_ref, k_ref, v_ref, p_ref, h_ref):
    for m in range(ENS):
        cols = slice(m * C, (m + 1) * C)
        q_ref[:, cols] = rz_ref[m, :, :C].astype(F32)
        k_ref[:, cols] = rz_ref[m, :, C : 2 * C].astype(F32)
        v_ref[:, cols] = rz_ref[m, :, 2 * C : 3 * C].astype(F32)
    mixed = rz_ref[0, :, 3 * C :].astype(F32)
    for m in range(1, ENS):
        mixed += rz_ref[m, :, 3 * C :].astype(F32)
    h_ref[...] = mixed[:, VP : VP + VAR]
    p_ref[...] = dot(mixed[:, :VAR].astype(BF), wh_ref[...])


def local(x, grid, edges, target, area, var, wq, wk, wv, wo, wh):
    vmem = pl.BlockSpec(memory_space=pltpu.VMEM)
    anywhere = pl.BlockSpec(memory_space=pl.ANY)
    dma = pltpu.SemaphoreType.DMA
    widths = (2 * VP, C, 2 * C)
    scratch = [
        pltpu.VMEM((G, D), BF), pltpu.VMEM((VAR, G), F32), pltpu.VMEM((VAR, D), BF),
        *[pltpu.VMEM((D, D), BF)] * 4,
        pltpu.VMEM((VP, D), BF),
        pltpu.VMEM((ENS * N, D), BF), pltpu.VMEM((D, ENS * N), BF),
        pltpu.VMEM((D, G), BF), pltpu.VMEM((2 * D, G), BF),
        pltpu.VMEM((G, D), BF), pltpu.VMEM((N, D), BF), pltpu.VMEM((N, D), BF),
        pltpu.VMEM((G, D), BF), pltpu.VMEM((G, D), BF),
        pltpu.VMEM((ENS, G, VP), BF), pltpu.VMEM((D, 2 * C), BF),
        pltpu.VMEM((PAIRS, E, W), BF), pltpu.VMEM((PAIRS, E, W), BF),
        pltpu.VMEM((PAIRS, E, W), F32), pltpu.VMEM((PAIRS, E, W), BF),
        pltpu.VMEM((ENS * G, VP), BF), pltpu.VMEM((PAIRS, G, W), BF),
        pltpu.VMEM((ENS * N, C), BF), pltpu.VMEM((ENS * N, C), BF),
        pltpu.VMEM((E, N), BF), pltpu.VMEM((N, E), BF),
        pltpu.VMEM((E, W), BF), pltpu.VMEM((G, C), F32), pltpu.VMEM((VP, C), BF),
        pltpu.VMEM((G, VP), F32), pltpu.VMEM((G, VP), F32),
        *[pltpu.VMEM((2, D // 2, w), BF) for w in widths],
        *[pltpu.VMEM((D // 2, w), BF) for w in widths],
        *[pltpu.VMEM((D // 2, w), BF) for w in widths],
        *[pltpu.VMEM((CHIPS, ROWS, w), BF) for w in widths],
        pltpu.VMEM((ENS, ROWS, 3 * C + 2 * VP), BF),
        dma((8,)), dma((8,)), dma((8,)), dma((ENS, 2)), dma((ENS,)), dma((ENS,)),
        dma((ENS,)), dma((ENS,)), dma((3,)), dma((3,)), dma((3, CHIPS)), dma((3, CHIPS)),
        dma((3, ENS)), dma((3, ENS)),
    ]
    rz = pl.pallas_call(
        main_kernel,
        out_shape=jax.ShapeDtypeStruct((ENS, ROWS, 3 * C + 2 * VP), BF),
        in_specs=[anywhere, anywhere, vmem, anywhere, vmem, vmem] + [anywhere] * 5,
        out_specs=anywhere,
        scratch_shapes=scratch,
        compiler_params=pltpu.CompilerParams(
            collective_id=0, has_side_effects=True, vmem_limit_bytes=56 << 20
        ),
        name="ensemble_gradients",
    )(x[0], grid, edges.T, target.T, area.reshape(1, G), var.reshape(1, VAR), wq, wk, wv, wo, wh.T)
    full = jax.ShapeDtypeStruct((ROWS, D), F32)
    return pl.pallas_call(
        finish_kernel,
        out_shape=(full, full, full, full, jax.ShapeDtypeStruct((ROWS, VAR), F32)),
        in_specs=[vmem, vmem],
        out_specs=(vmem,) * 5,
        name="finish",
    )(rz, wh.T)


def solution(mesh):
    in_specs = (
        P("ens", "space", None),
        P("space", None),
        P("space", None),
        P("space", None),
        P("space"),
        P(),
        P(),
        P(),
        P(),
        P(),
        P(),
    )
    out_specs = (P("space", None),) * 5
    return jax.shard_map(local, mesh=mesh, in_specs=in_specs, out_specs=out_specs, check_vma=False)
```

```python
import functools

import jax
import jax.numpy as jnp
from jax import lax
from jax.experimental import pallas as pl
from jax.experimental.pallas import tpu as pltpu
from jax.sharding import PartitionSpec as P

MESH = pl.DeviceIdType.MESH
HEADS = 16
KNN = 3
FAIR_ALPHA = 0.95
SMOOTH_SQ = 0.0625
ENS = 8
SPACE = 32
CX = 4
CY = 4
CHIPS = CX * CY
D = 1024
HD = D // HEADS
G = 256
M = 64
N = 3 * M
E = KNN * G
VAR = 100
VP = 128
C = D // ENS
ROWS = D // SPACE
W = 256
PAIRS = ENS // 2
BF = jnp.bfloat16
F32 = jnp.float32


def dot(a, b):
    return jnp.dot(a, b, preferred_element_type=F32)


def dot_nt(a, b):
    return lax.dot_general(a, b, (((1,), (1,)), ((), ())), preferred_element_type=F32)


def slope(d):
    return d * lax.rsqrt(d * d + SMOOTH_SQ)


def same_head(width, value):
    rows = lax.broadcasted_iota(jnp.int32, (width, width), 0) // HD
    cols = lax.broadcasted_iota(jnp.int32, (width, width), 1) // HD
    return jnp.where(rows == cols, value, 0.0).astype(BF)


def softmax3(scores):
    s0, s1, s2 = scores[:G], scores[G : 2 * G], scores[2 * G :]
    top = jnp.maximum(jnp.maximum(s0, s1), s2)
    e0, e1, e2 = jnp.exp(s0 - top), jnp.exp(s1 - top), jnp.exp(s2 - top)
    inv = 1.0 / (e0 + e1 + e2)
    return e0 * inv, e1 * inv, e2 * inv


def three(x):
    return jnp.concatenate([x, x, x], axis=0)


def side(x, y):
    return jnp.concatenate([x, y], axis=1)


PLACE = {0: 0, -1: 1, 1: 2, -2: 3, 2: 4, -3: 5, 3: 6, -4: 7, 4: 7}


def main_kernel(
    x_hbm, grid_hbm, edge_ref, target_hbm, area_ref, var_ref,
    wq_hbm, wk_hbm, wv_hbm, wo_hbm, wh_hbm,
    out_hbm,
    grid_ref, target_ref, wh_ref, wq, wk, wv, wo, wht, lat, lat_t, grid_t, mix_t, q, keys, values, attended, hidden,
    delta, wkvc, kg, vg, att_all, att_low, gl, ga, s_v, s_k, oh, oh_t, q3, gq, uct, common, areaw,
    part_ab, part_v, part_qk, sib_ab, sib_v, sib_qk, sum_ab, sum_v, sum_qk, r_ab, r_v, r_qk, rz,
    wsem, ring_s, ring_r, halo_s, halo_l, halo_r, d_s, d_r, sib_s, sib_r, xy_s, xy_r, z_s, z_r,
):
    e = lax.axis_index("ens")
    s = lax.axis_index("space")
    core = lax.rem(s, 2)
    chip_x = lax.rem(s // 2, CX)
    chip_y = s // (2 * CX)

    def ens_peer(d):
        return (lax.rem(e + d + ENS, ENS), s)

    def space_peer(d):
        return (e, lax.rem(s + d + SPACE, SPACE))

    def chip_peer(t):
        return lax.rem(chip_y + t // CX, CY) * CX + lax.rem(chip_x + lax.rem(t, CX), CX)

    sibling = (e, s + 1 - 2 * core)

    barrier = pltpu.get_barrier_semaphore()

    def greet(peer):
        pl.semaphore_signal(barrier, inc=1, device_id=peer, device_id_type=MESH)

    greet(space_peer(1))
    greet(space_peer(-1))

    @pl.loop(1, ENS)
    def _(d):
        greet(ens_peer(d))

    @pl.loop(1, CHIPS)
    def _(t):
        greet((e, chip_peer(t) * 2 + core))

    def own_rows(i):
        return pl.ds(i * N + M, M)

    def load(i, src, dst):
        copy = pltpu.make_async_copy(src, dst, wsem.at[i])
        copy.start()
        return copy

    load_x = load(0, x_hbm, lat.at[own_rows(0)])
    load_grid = load(1, grid_hbm, grid_ref)
    load_wq = load(2, wq_hbm, wq)
    loads = [
        load(i + 3, src, dst)
        for i, (src, dst) in enumerate(
            ((wh_hbm, wh_ref), (wk_hbm, wk), (wv_hbm, wv), (wo_hbm, wo), (target_hbm, target_ref))
        )
    ]

    def ring_copy(step, way, half):
        src = pl.ds(PLACE[(1 - step) * way] * N + M + half * (M // 2), M // 2)
        dst = pl.ds(PLACE[-step * way] * N + M + half * (M // 2), M // 2)
        sem = (step - 1) * 4 + (1 - way) + half
        return pltpu.make_async_remote_copy(
            src_ref=lat.at[src], dst_ref=lat.at[dst], send_sem=ring_s.at[sem], recv_sem=ring_r.at[sem],
            device_id=ens_peer(way), device_id_type=MESH,
        )

    ring = {(k, w, h): ring_copy(k, w, h) for k in range(1, 4) for h in (0, 1) for w in (1, -1)}
    ring[4, 1, 0] = ring_copy(4, 1, 0)
    ring[4, -1, 1] = ring_copy(4, -1, 1)

    def pass_on(step, half):
        for way in (1, -1):
            if (step, way, half) in ring:
                ring[step, way, half].wait_recv()
            if (step + 1, way, half) in ring:
                ring[step + 1, way, half].start()

    def halo_copies(i):
        up = pltpu.make_async_remote_copy(
            src_ref=lat.at[own_rows(i)], dst_ref=lat.at[pl.ds(i * N, M)],
            send_sem=halo_s.at[i, 0], recv_sem=halo_l.at[i],
            device_id=space_peer(1), device_id_type=MESH,
        )
        down = pltpu.make_async_remote_copy(
            src_ref=lat.at[own_rows(i)], dst_ref=lat.at[pl.ds(i * N + 2 * M, M)],
            send_sem=halo_s.at[i, 1], recv_sem=halo_r.at[i],
            device_id=space_peer(-1), device_id_type=MESH,
        )
        return up, down

    def start_halo(i):
        for copy in halo_copies(i):
            copy.start()

    def wait_halo(i):
        for copy in halo_copies(i):
            copy.wait_recv()

    load_grid.wait()
    load_wq.wait()
    for n in range(D // W):
        cols = slice(n * W, (n + 1) * W)
        q[:, cols] = dot(grid_ref[...], wq[:, cols]).astype(BF)

    load_x.wait()
    pl.semaphore_wait(barrier, 2 + ENS - 1 + CHIPS - 1)
    start_halo(0)
    for half in (0, 1):
        ring[1, 1, half].start()
        ring[1, -1, half].start()

    for copy in loads:
        copy.wait()
    wht[...] = jnp.zeros_like(wht)
    wht[:VAR, :] = wh_ref[...]
    edges = edge_ref[...]
    slot_rows = (((edges // M) - s + 1 + SPACE) % SPACE) * M + edges % M
    node = lax.broadcasted_iota(jnp.int32, (N, G), 0)
    for j in range(KNN):
        oh_t[:, j * G : (j + 1) * G] = jnp.where(slot_rows[j : j + 1, :] == node, 1.0, 0.0).astype(BF)
    oh[...] = oh_t[...].T
    grid_t[...] = grid_ref[...].T
    var_row = jnp.concatenate([var_ref[...], jnp.zeros((1, VP - VAR), F32)], axis=1)
    areaw[...] = jnp.broadcast_to(area_ref[...], (VP, G)).T * var_row
    common[...] = dot_nt(grid_ref[...], wht[...])
    hs = pl.ds(pl.multiple_of(e * C, C), C)
    wkvc[:, :C] = wk[:, hs]
    wkvc[:, C:] = wv[:, hs]
    uct[...] = dot_nt(wht[...], wo[hs, :]).astype(BF)
    q3[...] = three(side(q[:, hs], q[:, hs]))

    wait_halo(0)
    pass_on(1, 0)
    for n in range(D // W):
        cols = slice(n * W, (n + 1) * W)
        keys[:, cols] = dot(lat[:N, :], wk[:, cols]).astype(BF)
        values[:, cols] = dot(lat[:N, :], wv[:, cols]).astype(BF)
        if n == 1:
            pass_on(1, 1)
            start_halo(PLACE[-1])
            start_halo(PLACE[1])

    head_sum = same_head(W, HD**-0.5)
    for n in range(D // W):
        cols = slice(n * W, (n + 1) * W)
        prod = dot(oh[...], keys[:, cols]).astype(BF) * three(q[:, cols])
        att = softmax3(dot(prod, head_sum))
        value_rows = dot(oh[...], values[:, cols])
        total = jnp.zeros((G, W), F32)
        for j in range(KNN):
            total += att[j].astype(BF).astype(F32) * value_rows[j * G : (j + 1) * G]
        attended[:, cols] = total.astype(BF)
        if n == 1:
            pass_on(2, 0)

    pass_on(2, 1)
    start_halo(PLACE[-2])
    start_halo(PLACE[2])
    for n in range(D // W):
        cols = slice(n * W, (n + 1) * W)
        update = dot(attended[...], wo[:, cols])
        hidden[:, cols] = (grid_ref[:, cols].astype(F32) + update).astype(BF)

    delta[0] = (dot_nt(hidden[...], wht[...]) - common[...]).astype(BF)

    def delta_copy(sem, d_from, d_to, way, rows=slice(None)):
        return pltpu.make_async_remote_copy(
            src_ref=delta.at[PLACE[d_from], rows], dst_ref=delta.at[PLACE[d_to], rows],
            send_sem=d_s.at[sem], recv_sem=d_r.at[sem],
            device_id=ens_peer(way), device_id_type=MESH,
        )

    halves = (pl.ds(0, G // 2), pl.ds(G // 2, G // 2))
    near2 = {(w, h): delta_copy(1 - w + h, 0, -2 * w, 2 * w, halves[h]) for h in (0, 1) for w in (1, -1)}
    near1 = {w: delta_copy(4 + (1 - w) // 2, 0, -w, w) for w in (1, -1)}
    far3 = {(w, h): delta_copy(6 + 1 - w + h, -2 * w, -3 * w, w, halves[h]) for h in (0, 1) for w in (1, -1)}
    far4 = {w: delta_copy(10 + (1 - w) // 2, -2 * w, 4, 2 * w, halves[(1 - w) // 2]) for w in (1, -1)}
    deltas = [*near2.values(), *near1.values(), *far3.values(), *far4.values()]
    for copy in [*near2.values(), *near1.values()]:
        copy.start()

    def pass_delta_on(half):
        for way in (1, -1):
            near2[way, half].wait_recv()
            if half == (1 - way) // 2:
                far4[way].start()
            far3[way, half].start()

    def prepare(p):
        rows = slice(2 * p * N, 2 * (p + 1) * N)
        kv = dot(lat[rows, :], wkvc[...]).astype(BF)
        kg[p] = dot(oh[...], side(kv[:N, :C], kv[N:, :C])).astype(BF)
        vg[p] = dot(oh[...], side(kv[:N, C:], kv[N:, C:])).astype(BF)
        att = softmax3(dot(kg[p] * q3[...], head_sum))
        for j in range(KNN):
            att_all[p, j * G : (j + 1) * G, :] = att[j]
            att_low[p, j * G : (j + 1) * G, :] = att[j].astype(BF)
        lat_t[:, rows] = lat[rows, :].T

    padded = jnp.concatenate([target_ref[...], jnp.zeros((VP - VAR, G), F32)], axis=0)
    common[...] = common[...] - padded.T
    mix_t[:D, :] = attended[...].T
    pass_on(3, 0)
    wait_halo(1)
    prepare(0)
    pass_on(3, 1)
    start_halo(PLACE[-3])
    start_halo(PLACE[3])
    mix_t[D:, :] = hidden[...].T
    pass_delta_on(0)
    wait_halo(2)
    wait_halo(3)
    prepare(1)
    pass_delta_on(1)
    pass_on(4, 0)
    pass_on(4, 1)
    start_halo(PLACE[4])
    wait_halo(4)
    wait_halo(5)
    prepare(2)
    wait_halo(6)
    wait_halo(7)
    prepare(3)

    for copy in [*near1.values(), *far3.values(), *far4.values()]:
        copy.wait_recv()

    fair_eps = (1.0 - FAIR_ALPHA) / ENS
    pair_coef = (1.0 - fair_eps) / (ENS * (ENS - 1))
    step_rows = 16

    @pl.loop(0, G // step_rows)
    def _(i):
        rows = pl.ds(pl.multiple_of(i * step_rows, step_rows), step_rows)
        dev = [delta[m, rows, :].astype(F32) for m in range(ENS)]
        pair = [None] * ENS
        for a in range(ENS):
            for b in range(a + 1, ENS):
                t = slope(dev[a] - dev[b])
                pair[a] = t if pair[a] is None else pair[a] + t
                pair[b] = -t if pair[b] is None else pair[b] - t
        shift = common[rows, :]
        scale = areaw[rows, :]
        for m in range(ENS):
            grad = scale * (slope(dev[m] + shift) * (1.0 / ENS) - pair_coef * pair[m])
            gl[pl.ds(pl.multiple_of(m * G + i * step_rows, step_rows), step_rows), :] = grad.astype(BF)

    def sibling_copy(i, part, sib):
        return pltpu.make_async_remote_copy(
            src_ref=part.at[1 - core], dst_ref=sib, send_sem=sib_s.at[i], recv_sem=sib_r.at[i],
            device_id=sibling, device_id_type=MESH,
        )

    def chip_copy(i, summed, r, t):
        chip = chip_peer(t)
        return pltpu.make_async_remote_copy(
            src_ref=summed.at[pl.ds(pl.multiple_of(chip * ROWS, ROWS), ROWS)], dst_ref=r.at[t],
            send_sem=xy_s.at[i, t], recv_sem=xy_r.at[i, t],
            device_id=(e, chip * 2 + core), device_id_type=MESH,
        )

    def spread(i, part, sib, summed, r):
        sibling_copy(i, part, sib).wait_recv()
        summed[...] = (part[core].astype(F32) + sib[...].astype(F32)).astype(BF)

        @pl.loop(1, CHIPS)
        def _(t):
            chip_copy(i, summed, r, t).start()

        r[0] = summed[pl.ds(pl.multiple_of((s // 2) * ROWS, ROWS), ROWS), :]

    def last_copy(i, cols, d, m):
        return pltpu.make_async_remote_copy(
            src_ref=rz.at[e, :, cols], dst_ref=rz.at[m, :, cols],
            send_sem=z_s.at[i, d], recv_sem=z_r.at[i, m],
            device_id=ens_peer(d), device_id_type=MESH,
        )

    def collect(i, summed, r, cols):
        @pl.loop(1, CHIPS)
        def _(t):
            chip_copy(i, summed, r, t).wait_recv()

        rz[e, :, cols] = jnp.sum(r[...].astype(F32), axis=0).astype(BF)

        for d in (4, 3, 5, 2, 6, 1, 7):
            last_copy(i, cols, d, e).start()

    def put(part, chunk, cols, value):
        value = value.astype(BF)
        for k in range(W // ROWS):
            dest = chunk * (W // ROWS) + k
            rows = slice((dest // 2) * ROWS, (dest // 2 + 1) * ROWS)
            part[dest % 2, rows, cols] = value[k * ROWS : (k + 1) * ROWS, :]

    ab, v, qk = (0, part_ab, sib_ab), (1, part_v, sib_v), (2, part_qk, sib_qk)
    for i in range(D // W):
        rows = slice(i * W, (i + 1) * W)
        put(part_ab, i, slice(0, VP), dot(mix_t[rows, :], gl[:G, :]))
        put(part_ab, i, slice(VP, 2 * VP), dot(mix_t[D + i * W : D + (i + 1) * W, :], gl[:G, :]))
    sibling_copy(*ab).start()

    for p in range(PAIRS):
        rows = slice(p * 2 * G, (p + 1) * 2 * G)
        both = dot(gl[rows, :], uct[...]).astype(BF)
        both = side(both[:G], both[G:])
        ga[p] = both
        sums = dot(oh_t[...], att_low[p] * three(both)).astype(BF)
        s_v[2 * p * N : (2 * p + 1) * N, :] = sums[:, :C]
        s_v[(2 * p + 1) * N : (2 * p + 2) * N, :] = sums[:, C:]

    for i in range(D // W):
        put(part_v, i, slice(0, C), dot(lat_t[i * W : (i + 1) * W, :], s_v[...]))
    sibling_copy(*v).start()
    spread(*ab, sum_ab, r_ab)

    gq[...] = jnp.zeros_like(gq)
    ones = same_head(W, 1.0)

    for p in range(PAIRS):
        gw = dot(vg[p] * three(ga[p]), ones)
        att = att_all[p]
        t = att * gw
        gs = (att * (gw - three(t[:G] + t[G : 2 * G] + t[2 * G :])) * HD**-0.5).astype(BF)
        gqe = gs.astype(F32) * kg[p].astype(F32)
        gqe = gqe[:G] + gqe[G : 2 * G] + gqe[2 * G :]
        gq[...] += gqe[:, :C] + gqe[:, C:]
        sums = dot(oh_t[...], gs * q3[...]).astype(BF)
        s_k[2 * p * N : (2 * p + 1) * N, :] = sums[:, :C]
        s_k[(2 * p + 1) * N : (2 * p + 2) * N, :] = sums[:, C:]

    spread(*v, sum_v, r_v)
    for i in range(D // W):
        rows = slice(i * W, (i + 1) * W)
        put(part_qk, i, slice(0, C), dot(grid_t[rows, :], gq[...].astype(BF)))
        put(part_qk, i, slice(C, 2 * C), dot(lat_t[rows, :], s_k[...]))
    sibling_copy(*qk).start()
    qk_cols, v_cols, ab_cols = slice(0, 2 * C), slice(2 * C, 3 * C), slice(3 * C, 3 * C + 2 * VP)
    spread(*qk, sum_qk, r_qk)
    collect(0, sum_ab, r_ab, ab_cols)
    collect(1, sum_v, r_v, v_cols)
    collect(2, sum_qk, r_qk, qk_cols)

    for copy in [*ring.values(), *deltas]:
        copy.wait_send()
    for i in range(ENS):
        for copy in halo_copies(i):
            copy.wait_send()
    stores = []
    for i, summed, r, cols in ((0, sum_ab, r_ab, ab_cols), (1, sum_v, r_v, v_cols), (2, sum_qk, r_qk, qk_cols)):
        sibling_copy(*(ab, v, qk)[i]).wait_send()

        @pl.loop(1, CHIPS)
        def _(t, i=i, summed=summed, r=r):
            chip_copy(i, summed, r, t).wait_send()

        @pl.loop(1, ENS)
        def _(d, i=i, cols=cols):
            last_copy(i, cols, d, e).wait_send()
            last_copy(i, cols, d, lax.rem(e + d, ENS)).wait_recv()

        stores.append(pltpu.make_async_copy(rz.at[:, :, cols], out_hbm.at[:, :, cols], wsem.at[i]))
        stores[-1].start()
    for store in stores:
        store.wait()


def finish_kernel(rz_ref, wh_ref, q_ref, k_ref, v_ref, p_ref, h_ref):
    for m in range(ENS):
        cols = slice(m * C, (m + 1) * C)
        q_ref[:, cols] = rz_ref[m, :, :C].astype(F32)
        k_ref[:, cols] = rz_ref[m, :, C : 2 * C].astype(F32)
        v_ref[:, cols] = rz_ref[m, :, 2 * C : 3 * C].astype(F32)
    mixed = rz_ref[0, :, 3 * C :].astype(F32)
    for m in range(1, ENS):
        mixed += rz_ref[m, :, 3 * C :].astype(F32)
    h_ref[...] = mixed[:, VP : VP + VAR]
    p_ref[...] = dot(mixed[:, :VAR].astype(BF), wh_ref[...])


def local(x, grid, edges, target, area, var, wq, wk, wv, wo, wh):
    vmem = pl.BlockSpec(memory_space=pltpu.VMEM)
    anywhere = pl.BlockSpec(memory_space=pl.ANY)
    dma = pltpu.SemaphoreType.DMA
    widths = (2 * VP, C, 2 * C)
    scratch = [
        pltpu.VMEM((G, D), BF), pltpu.VMEM((VAR, G), F32), pltpu.VMEM((VAR, D), BF),
        *[pltpu.VMEM((D, D), BF)] * 4,
        pltpu.VMEM((VP, D), BF),
        pltpu.VMEM((ENS * N, D), BF), pltpu.VMEM((D, ENS * N), BF),
        pltpu.VMEM((D, G), BF), pltpu.VMEM((2 * D, G), BF),
        pltpu.VMEM((G, D), BF), pltpu.VMEM((N, D), BF), pltpu.VMEM((N, D), BF),
        pltpu.VMEM((G, D), BF), pltpu.VMEM((G, D), BF),
        pltpu.VMEM((ENS, G, VP), BF), pltpu.VMEM((D, 2 * C), BF),
        pltpu.VMEM((PAIRS, E, W), BF), pltpu.VMEM((PAIRS, E, W), BF),
        pltpu.VMEM((PAIRS, E, W), F32), pltpu.VMEM((PAIRS, E, W), BF),
        pltpu.VMEM((ENS * G, VP), BF), pltpu.VMEM((PAIRS, G, W), BF),
        pltpu.VMEM((ENS * N, C), BF), pltpu.VMEM((ENS * N, C), BF),
        pltpu.VMEM((E, N), BF), pltpu.VMEM((N, E), BF),
        pltpu.VMEM((E, W), BF), pltpu.VMEM((G, C), F32), pltpu.VMEM((VP, C), BF),
        pltpu.VMEM((G, VP), F32), pltpu.VMEM((G, VP), F32),
        *[pltpu.VMEM((2, D // 2, w), BF) for w in widths],
        *[pltpu.VMEM((D // 2, w), BF) for w in widths],
        *[pltpu.VMEM((D // 2, w), BF) for w in widths],
        *[pltpu.VMEM((CHIPS, ROWS, w), BF) for w in widths],
        pltpu.VMEM((ENS, ROWS, 3 * C + 2 * VP), BF),
        dma((8,)), dma((16,)), dma((16,)), dma((ENS, 2)), dma((ENS,)), dma((ENS,)),
        dma((12,)), dma((12,)), dma((3,)), dma((3,)), dma((3, CHIPS)), dma((3, CHIPS)),
        dma((3, ENS)), dma((3, ENS)),
    ]
    rz = pl.pallas_call(
        main_kernel,
        out_shape=jax.ShapeDtypeStruct((ENS, ROWS, 3 * C + 2 * VP), BF),
        in_specs=[anywhere, anywhere, vmem, anywhere, vmem, vmem] + [anywhere] * 5,
        out_specs=anywhere,
        scratch_shapes=scratch,
        compiler_params=pltpu.CompilerParams(
            collective_id=0, has_side_effects=True, vmem_limit_bytes=56 << 20
        ),
        name="ensemble_gradients",
    )(x[0], grid, edges.T, target.T, area.reshape(1, G), var.reshape(1, VAR), wq, wk, wv, wo, wh.T)
    full = jax.ShapeDtypeStruct((ROWS, D), F32)
    return pl.pallas_call(
        finish_kernel,
        out_shape=(full, full, full, full, jax.ShapeDtypeStruct((ROWS, VAR), F32)),
        in_specs=[vmem, vmem],
        out_specs=(vmem,) * 5,
        name="finish",
    )(rz, wh.T)


def solution(mesh):
    in_specs = (
        P("ens", "space", None),
        P("space", None),
        P("space", None),
        P("space", None),
        P("space"),
        P(),
        P(),
        P(),
        P(),
        P(),
        P(),
    )
    out_specs = (P("space", None),) * 5
    return jax.shard_map(local, mesh=mesh, in_specs=in_specs, out_specs=out_specs, check_vma=False)
```

```python
import functools

import jax
import jax.numpy as jnp
from jax import lax
from jax.experimental import pallas as pl
from jax.experimental.pallas import tpu as pltpu
from jax.sharding import PartitionSpec as P

MESH = pl.DeviceIdType.MESH
HEADS = 16
KNN = 3
FAIR_ALPHA = 0.95
SMOOTH_SQ = 0.0625
ENS = 8
SPACE = 32
CX = 4
CY = 4
CHIPS = CX * CY
D = 1024
HD = D // HEADS
G = 256
M = 64
N = 3 * M
E = KNN * G
VAR = 100
VP = 128
C = D // ENS
ROWS = D // SPACE
W = 256
PAIRS = ENS // 2
BF = jnp.bfloat16
F32 = jnp.float32


def dot(a, b):
    return jnp.dot(a, b, preferred_element_type=F32)


def dot_nt(a, b):
    return lax.dot_general(a, b, (((1,), (1,)), ((), ())), preferred_element_type=F32)


def slope(d):
    return d * lax.rsqrt(d * d + SMOOTH_SQ)


def same_head(width, value):
    rows = lax.broadcasted_iota(jnp.int32, (width, width), 0) // HD
    cols = lax.broadcasted_iota(jnp.int32, (width, width), 1) // HD
    return jnp.where(rows == cols, value, 0.0).astype(BF)


def softmax3(scores):
    s0, s1, s2 = scores[:G], scores[G : 2 * G], scores[2 * G :]
    top = jnp.maximum(jnp.maximum(s0, s1), s2)
    e0, e1, e2 = jnp.exp(s0 - top), jnp.exp(s1 - top), jnp.exp(s2 - top)
    inv = 1.0 / (e0 + e1 + e2)
    return e0 * inv, e1 * inv, e2 * inv


def three(x):
    return jnp.concatenate([x, x, x], axis=0)


def side(x, y):
    return jnp.concatenate([x, y], axis=1)


PLACE = {0: 0, -1: 1, 1: 2, -2: 3, 2: 4, -3: 5, 3: 6, -4: 7, 4: 7}


FAR_FIRST = sorted(range(1, CHIPS), key=lambda t: -min(t // CX, CY - t // CX) - min(t % CX, CX - t % CX))


def main_kernel(
    x_hbm, grid_hbm, edge_ref, target_hbm, area_ref, var_ref,
    wq_hbm, wk_hbm, wv_hbm, wo_hbm, wh_hbm,
    out_hbm,
    grid_ref, target_ref, wh_ref, wq, wk, wv, wo, wht, lat, lat_t, grid_t, mix_t, q, keys, values, attended, hidden,
    delta, wkvc, kg, vg, att_all, att_low, gl, ga, s_v, s_k, oh, oh_t, q3, gq, uct, common, areaw,
    part_ab, part_v, part_qk, sib_ab, sib_v, sib_qk, sum_ab, sum_v, sum_qk, r_ab, r_v, r_qk, rz,
    wsem, ring_s, ring_r, halo_s, halo_l, halo_r, d_s, d_r, sib_s, sib_r, xy_s, xy_r, z_s, z_r, tokens,
):
    e = lax.axis_index("ens")
    s = lax.axis_index("space")
    core = lax.rem(s, 2)
    chip_x = lax.rem(s // 2, CX)
    chip_y = s // (2 * CX)

    def ens_peer(d):
        return (lax.rem(e + d + ENS, ENS), s)

    def space_peer(d):
        return (e, lax.rem(s + d + SPACE, SPACE))

    def chip_peer(t):
        return lax.rem(chip_y + t // CX, CY) * CX + lax.rem(chip_x + lax.rem(t, CX), CX)

    sibling = (e, s + 1 - 2 * core)

    barrier = pltpu.get_barrier_semaphore()

    def greet(peer):
        pl.semaphore_signal(barrier, inc=1, device_id=peer, device_id_type=MESH)

    along_x = [(e, chip_peer(1) * 2 + core), (e, chip_peer(CX - 1) * 2 + core)]
    along_y = [(e, chip_peer(CX) * 2 + core), (e, chip_peer((CY - 1) * CX) * 2 + core)]
    neighbours = [space_peer(1), space_peer(-1), ens_peer(1), ens_peer(-1), *along_x, *along_y]
    for peer in neighbours:
        greet(peer)

    def give_token(i):
        for peer in along_x if i == 0 else along_y:
            pl.semaphore_signal(tokens.at[i], inc=1, device_id=peer, device_id_type=MESH)

    def take_token(i):
        pl.semaphore_wait(tokens.at[i], 2)

    def own_rows(i):
        return pl.ds(i * N + M, M)

    def load(i, src, dst):
        copy = pltpu.make_async_copy(src, dst, wsem.at[i])
        copy.start()
        return copy

    load_x = load(0, x_hbm, lat.at[own_rows(0)])
    load_grid = load(1, grid_hbm, grid_ref)
    load_wq = load(2, wq_hbm, wq)
    loads = [
        load(i + 3, src, dst)
        for i, (src, dst) in enumerate(
            ((wh_hbm, wh_ref), (wk_hbm, wk), (wv_hbm, wv), (wo_hbm, wo), (target_hbm, target_ref))
        )
    ]

    def ring_copy(step, way, half):
        src = pl.ds(PLACE[(1 - step) * way] * N + M + half * (M // 2), M // 2)
        dst = pl.ds(PLACE[-step * way] * N + M + half * (M // 2), M // 2)
        sem = (step - 1) * 4 + (1 - way) + half
        return pltpu.make_async_remote_copy(
            src_ref=lat.at[src], dst_ref=lat.at[dst], send_sem=ring_s.at[sem], recv_sem=ring_r.at[sem],
            device_id=ens_peer(way), device_id_type=MESH,
        )

    ring = {(k, w, h): ring_copy(k, w, h) for k in range(1, 4) for h in (0, 1) for w in (1, -1)}
    ring[4, 1, 0] = ring_copy(4, 1, 0)
    ring[4, -1, 1] = ring_copy(4, -1, 1)

    def pass_on(step, half):
        for way in (1, -1):
            if (step, way, half) in ring:
                ring[step, way, half].wait_recv()
            if (step + 1, way, half) in ring:
                ring[step + 1, way, half].start()

    def halo_copies(i):
        up = pltpu.make_async_remote_copy(
            src_ref=lat.at[own_rows(i)], dst_ref=lat.at[pl.ds(i * N, M)],
            send_sem=halo_s.at[i, 0], recv_sem=halo_l.at[i],
            device_id=space_peer(1), device_id_type=MESH,
        )
        down = pltpu.make_async_remote_copy(
            src_ref=lat.at[own_rows(i)], dst_ref=lat.at[pl.ds(i * N + 2 * M, M)],
            send_sem=halo_s.at[i, 1], recv_sem=halo_r.at[i],
            device_id=space_peer(-1), device_id_type=MESH,
        )
        return up, down

    def start_halo(i):
        for copy in halo_copies(i):
            copy.start()

    def wait_halo(i):
        for copy in halo_copies(i):
            copy.wait_recv()

    load_grid.wait()
    load_wq.wait()
    for n in range(D // W):
        cols = slice(n * W, (n + 1) * W)
        q[:, cols] = dot(grid_ref[...], wq[:, cols]).astype(BF)

    load_x.wait()
    pl.semaphore_wait(barrier, len(neighbours))
    start_halo(0)
    for half in (0, 1):
        ring[1, 1, half].start()
        ring[1, -1, half].start()
    give_token(0)

    for copy in loads:
        copy.wait()
    wht[...] = jnp.zeros_like(wht)
    wht[:VAR, :] = wh_ref[...]
    edges = edge_ref[...]
    slot_rows = (((edges // M) - s + 1 + SPACE) % SPACE) * M + edges % M
    node = lax.broadcasted_iota(jnp.int32, (N, G), 0)
    for j in range(KNN):
        oh_t[:, j * G : (j + 1) * G] = jnp.where(slot_rows[j : j + 1, :] == node, 1.0, 0.0).astype(BF)
    oh[...] = oh_t[...].T
    grid_t[...] = grid_ref[...].T
    var_row = jnp.concatenate([var_ref[...], jnp.zeros((1, VP - VAR), F32)], axis=1)
    areaw[...] = jnp.broadcast_to(area_ref[...], (VP, G)).T * var_row
    common[...] = dot_nt(grid_ref[...], wht[...])
    hs = pl.ds(pl.multiple_of(e * C, C), C)
    wkvc[:, :C] = wk[:, hs]
    wkvc[:, C:] = wv[:, hs]
    uct[...] = dot_nt(wht[...], wo[hs, :]).astype(BF)
    q3[...] = three(side(q[:, hs], q[:, hs]))

    wait_halo(0)
    pass_on(1, 0)
    take_token(0)
    give_token(1)
    for n in range(D // W):
        cols = slice(n * W, (n + 1) * W)
        keys[:, cols] = dot(lat[:N, :], wk[:, cols]).astype(BF)
        values[:, cols] = dot(lat[:N, :], wv[:, cols]).astype(BF)
        if n == 1:
            pass_on(1, 1)
            start_halo(PLACE[-1])
            start_halo(PLACE[1])

    head_sum = same_head(W, HD**-0.5)
    for n in range(D // W):
        cols = slice(n * W, (n + 1) * W)
        prod = dot(oh[...], keys[:, cols]).astype(BF) * three(q[:, cols])
        att = softmax3(dot(prod, head_sum))
        value_rows = dot(oh[...], values[:, cols])
        total = jnp.zeros((G, W), F32)
        for j in range(KNN):
            total += att[j].astype(BF).astype(F32) * value_rows[j * G : (j + 1) * G]
        attended[:, cols] = total.astype(BF)
        if n == 1:
            pass_on(2, 0)
            take_token(1)
            give_token(2)

    pass_on(2, 1)
    start_halo(PLACE[-2])
    start_halo(PLACE[2])
    for n in range(D // W):
        cols = slice(n * W, (n + 1) * W)
        update = dot(attended[...], wo[:, cols])
        hidden[:, cols] = (grid_ref[:, cols].astype(F32) + update).astype(BF)

    delta[0] = (dot_nt(hidden[...], wht[...]) - common[...]).astype(BF)

    def delta_copy(sem, d_from, d_to, way, rows=slice(None)):
        return pltpu.make_async_remote_copy(
            src_ref=delta.at[PLACE[d_from], rows], dst_ref=delta.at[PLACE[d_to], rows],
            send_sem=d_s.at[sem], recv_sem=d_r.at[sem],
            device_id=ens_peer(way), device_id_type=MESH,
        )

    halves = (pl.ds(0, G // 2), pl.ds(G // 2, G // 2))
    near2 = {(w, h): delta_copy(1 - w + h, 0, -2 * w, 2 * w, halves[h]) for h in (0, 1) for w in (1, -1)}
    near1 = {w: delta_copy(4 + (1 - w) // 2, 0, -w, w) for w in (1, -1)}
    far3 = {(w, h): delta_copy(6 + 1 - w + h, -2 * w, -3 * w, w, halves[h]) for h in (0, 1) for w in (1, -1)}
    far4 = {w: delta_copy(10 + (1 - w) // 2, -2 * w, 4, 2 * w, halves[(1 - w) // 2]) for w in (1, -1)}
    deltas = [*near2.values(), *near1.values(), *far3.values(), *far4.values()]
    for copy in [*near2.values(), *near1.values()]:
        copy.start()

    def pass_delta_on(half):
        for way in (1, -1):
            near2[way, half].wait_recv()
            if half == (1 - way) // 2:
                far4[way].start()
            far3[way, half].start()

    def prepare(p):
        rows = slice(2 * p * N, 2 * (p + 1) * N)
        kv = dot(lat[rows, :], wkvc[...]).astype(BF)
        kg[p] = dot(oh[...], side(kv[:N, :C], kv[N:, :C])).astype(BF)
        vg[p] = dot(oh[...], side(kv[:N, C:], kv[N:, C:])).astype(BF)
        att = softmax3(dot(kg[p] * q3[...], head_sum))
        for j in range(KNN):
            att_all[p, j * G : (j + 1) * G, :] = att[j]
            att_low[p, j * G : (j + 1) * G, :] = att[j].astype(BF)
        lat_t[:, rows] = lat[rows, :].T

    padded = jnp.concatenate([target_ref[...], jnp.zeros((VP - VAR, G), F32)], axis=0)
    common[...] = common[...] - padded.T
    mix_t[:D, :] = attended[...].T
    pass_on(3, 0)
    wait_halo(1)
    prepare(0)
    pass_on(3, 1)
    start_halo(PLACE[-3])
    start_halo(PLACE[3])
    mix_t[D:, :] = hidden[...].T
    pass_delta_on(0)
    wait_halo(2)
    wait_halo(3)
    prepare(1)
    pass_delta_on(1)
    pass_on(4, 0)
    pass_on(4, 1)
    start_halo(PLACE[4])
    wait_halo(4)
    wait_halo(5)
    prepare(2)
    wait_halo(6)
    wait_halo(7)
    prepare(3)

    for copy in [*near1.values(), *far3.values(), *far4.values()]:
        copy.wait_recv()
    take_token(2)

    fair_eps = (1.0 - FAIR_ALPHA) / ENS
    pair_coef = (1.0 - fair_eps) / (ENS * (ENS - 1))
    step_rows = 16

    @pl.loop(0, G // step_rows)
    def _(i):
        rows = pl.ds(pl.multiple_of(i * step_rows, step_rows), step_rows)
        dev = [delta[m, rows, :].astype(F32) for m in range(ENS)]
        pair = [None] * ENS
        for a in range(ENS):
            for b in range(a + 1, ENS):
                t = slope(dev[a] - dev[b])
                pair[a] = t if pair[a] is None else pair[a] + t
                pair[b] = -t if pair[b] is None else pair[b] - t
        shift = common[rows, :]
        scale = areaw[rows, :]
        for m in range(ENS):
            grad = scale * (slope(dev[m] + shift) * (1.0 / ENS) - pair_coef * pair[m])
            gl[pl.ds(pl.multiple_of(m * G + i * step_rows, step_rows), step_rows), :] = grad.astype(BF)

    def sibling_copy(i, part, sib):
        return pltpu.make_async_remote_copy(
            src_ref=part.at[1 - core], dst_ref=sib, send_sem=sib_s.at[i], recv_sem=sib_r.at[i],
            device_id=sibling, device_id_type=MESH,
        )

    def chip_copy(i, summed, r, t):
        chip = chip_peer(t)
        return pltpu.make_async_remote_copy(
            src_ref=summed.at[pl.ds(pl.multiple_of(chip * ROWS, ROWS), ROWS)], dst_ref=r.at[t],
            send_sem=xy_s.at[i, t], recv_sem=xy_r.at[i, t],
            device_id=(e, chip * 2 + core), device_id_type=MESH,
        )

    def spread(i, part, sib, summed, r):
        sibling_copy(i, part, sib).wait_recv()
        summed[...] = (part[core].astype(F32) + sib[...].astype(F32)).astype(BF)

        for t in FAR_FIRST:
            chip_copy(i, summed, r, t).start()

        r[0] = summed[pl.ds(pl.multiple_of((s // 2) * ROWS, ROWS), ROWS), :]

    def last_copy(i, cols, d, m):
        return pltpu.make_async_remote_copy(
            src_ref=rz.at[e, :, cols], dst_ref=rz.at[m, :, cols],
            send_sem=z_s.at[i, d], recv_sem=z_r.at[i, m],
            device_id=ens_peer(d), device_id_type=MESH,
        )

    def collect(i, summed, r, cols):
        @pl.loop(1, CHIPS)
        def _(t):
            chip_copy(i, summed, r, t).wait_recv()

        rz[e, :, cols] = jnp.sum(r[...].astype(F32), axis=0).astype(BF)

        for d in (4, 3, 5, 2, 6, 1, 7):
            last_copy(i, cols, d, e).start()

    def put(part, chunk, cols, value):
        value = value.astype(BF)
        for k in range(W // ROWS):
            dest = chunk * (W // ROWS) + k
            rows = slice((dest // 2) * ROWS, (dest // 2 + 1) * ROWS)
            part[dest % 2, rows, cols] = value[k * ROWS : (k + 1) * ROWS, :]

    ab, v, qk = (0, part_ab, sib_ab), (1, part_v, sib_v), (2, part_qk, sib_qk)
    for i in range(D // W):
        rows = slice(i * W, (i + 1) * W)
        put(part_ab, i, slice(0, VP), dot(mix_t[rows, :], gl[:G, :]))
        put(part_ab, i, slice(VP, 2 * VP), dot(mix_t[D + i * W : D + (i + 1) * W, :], gl[:G, :]))
    sibling_copy(*ab).start()

    for p in range(PAIRS):
        both = dot(gl[p * 2 * G : (p + 1) * 2 * G, :], uct[...]).astype(BF)
        ga[p] = side(both[:G], both[G:])

    def to_nodes(p, sums, s_ref):
        s_ref[2 * p * N : (2 * p + 1) * N, :] = sums[:, :C]
        s_ref[(2 * p + 1) * N : (2 * p + 2) * N, :] = sums[:, C:]

    ones = same_head(W, 1.0)
    for p in range(PAIRS):
        gw = dot(vg[p] * three(ga[p]), ones)
        att = att_all[p]
        t = att * gw
        gs = (att * (gw - three(t[:G] + t[G : 2 * G] + t[2 * G :])) * HD**-0.5).astype(BF)
        gqe = gs.astype(F32) * kg[p].astype(F32)
        gqe = gqe[:G] + gqe[G : 2 * G] + gqe[2 * G :]
        gqe = gqe[:, :C] + gqe[:, C:]
        gq[...] = gqe if p == 0 else gq[...] + gqe
        to_nodes(p, dot(oh_t[...], gs * q3[...]).astype(BF), s_k)
        if p == 1:
            spread(*ab, sum_ab, r_ab)

    for i in range(D // W):
        rows = slice(i * W, (i + 1) * W)
        put(part_qk, i, slice(0, C), dot(grid_t[rows, :], gq[...].astype(BF)))
        put(part_qk, i, slice(C, 2 * C), dot(lat_t[rows, :], s_k[...]))
    sibling_copy(*qk).start()
    for p in range(PAIRS):
        to_nodes(p, dot(oh_t[...], att_low[p] * three(ga[p])).astype(BF), s_v)
    spread(*qk, sum_qk, r_qk)
    for i in range(D // W):
        put(part_v, i, slice(0, C), dot(lat_t[i * W : (i + 1) * W, :], s_v[...]))
    sibling_copy(*v).start()
    qk_cols, v_cols, ab_cols = slice(0, 2 * C), slice(2 * C, 3 * C), slice(3 * C, 3 * C + 2 * VP)
    collect(0, sum_ab, r_ab, ab_cols)
    spread(*v, sum_v, r_v)
    collect(2, sum_qk, r_qk, qk_cols)
    collect(1, sum_v, r_v, v_cols)

    for copy in [*ring.values(), *deltas]:
        copy.wait_send()
    for i in range(ENS):
        for copy in halo_copies(i):
            copy.wait_send()
    stores = []
    for i, summed, r, cols in ((0, sum_ab, r_ab, ab_cols), (2, sum_qk, r_qk, qk_cols), (1, sum_v, r_v, v_cols)):
        sibling_copy(*(ab, v, qk)[i]).wait_send()

        @pl.loop(1, CHIPS)
        def _(t, i=i, summed=summed, r=r):
            chip_copy(i, summed, r, t).wait_send()

        @pl.loop(1, ENS)
        def _(d, i=i, cols=cols):
            last_copy(i, cols, d, e).wait_send()
            last_copy(i, cols, d, lax.rem(e + d, ENS)).wait_recv()

        stores.append(pltpu.make_async_copy(rz.at[:, :, cols], out_hbm.at[:, :, cols], wsem.at[i]))
        stores[-1].start()
    for store in stores:
        store.wait()


def finish_kernel(rz_ref, wh_ref, q_ref, k_ref, v_ref, p_ref, h_ref):
    for m in range(ENS):
        cols = slice(m * C, (m + 1) * C)
        q_ref[:, cols] = rz_ref[m, :, :C].astype(F32)
        k_ref[:, cols] = rz_ref[m, :, C : 2 * C].astype(F32)
        v_ref[:, cols] = rz_ref[m, :, 2 * C : 3 * C].astype(F32)
    mixed = rz_ref[0, :, 3 * C :].astype(F32)
    for m in range(1, ENS):
        mixed += rz_ref[m, :, 3 * C :].astype(F32)
    h_ref[...] = mixed[:, VP : VP + VAR]
    p_ref[...] = dot(mixed[:, :VAR].astype(BF), wh_ref[...])


def local(x, grid, edges, target, area, var, wq, wk, wv, wo, wh):
    vmem = pl.BlockSpec(memory_space=pltpu.VMEM)
    anywhere = pl.BlockSpec(memory_space=pl.ANY)
    dma = pltpu.SemaphoreType.DMA
    widths = (2 * VP, C, 2 * C)
    scratch = [
        pltpu.VMEM((G, D), BF), pltpu.VMEM((VAR, G), F32), pltpu.VMEM((VAR, D), BF),
        *[pltpu.VMEM((D, D), BF)] * 4,
        pltpu.VMEM((VP, D), BF),
        pltpu.VMEM((ENS * N, D), BF), pltpu.VMEM((D, ENS * N), BF),
        pltpu.VMEM((D, G), BF), pltpu.VMEM((2 * D, G), BF),
        pltpu.VMEM((G, D), BF), pltpu.VMEM((N, D), BF), pltpu.VMEM((N, D), BF),
        pltpu.VMEM((G, D), BF), pltpu.VMEM((G, D), BF),
        pltpu.VMEM((ENS, G, VP), BF), pltpu.VMEM((D, 2 * C), BF),
        pltpu.VMEM((PAIRS, E, W), BF), pltpu.VMEM((PAIRS, E, W), BF),
        pltpu.VMEM((PAIRS, E, W), F32), pltpu.VMEM((PAIRS, E, W), BF),
        pltpu.VMEM((ENS * G, VP), BF), pltpu.VMEM((PAIRS, G, W), BF),
        pltpu.VMEM((ENS * N, C), BF), pltpu.VMEM((ENS * N, C), BF),
        pltpu.VMEM((E, N), BF), pltpu.VMEM((N, E), BF),
        pltpu.VMEM((E, W), BF), pltpu.VMEM((G, C), F32), pltpu.VMEM((VP, C), BF),
        pltpu.VMEM((G, VP), F32), pltpu.VMEM((G, VP), F32),
        *[pltpu.VMEM((2, D // 2, w), BF) for w in widths],
        *[pltpu.VMEM((D // 2, w), BF) for w in widths],
        *[pltpu.VMEM((D // 2, w), BF) for w in widths],
        *[pltpu.VMEM((CHIPS, ROWS, w), BF) for w in widths],
        pltpu.VMEM((ENS, ROWS, 3 * C + 2 * VP), BF),
        dma((8,)), dma((16,)), dma((16,)), dma((ENS, 2)), dma((ENS,)), dma((ENS,)),
        dma((12,)), dma((12,)), dma((3,)), dma((3,)), dma((3, CHIPS)), dma((3, CHIPS)),
        dma((3, ENS)), dma((3, ENS)), pltpu.SemaphoreType.REGULAR((3,)),
    ]
    rz = pl.pallas_call(
        main_kernel,
        out_shape=jax.ShapeDtypeStruct((ENS, ROWS, 3 * C + 2 * VP), BF),
        in_specs=[anywhere, anywhere, vmem, anywhere, vmem, vmem] + [anywhere] * 5,
        out_specs=anywhere,
        scratch_shapes=scratch,
        compiler_params=pltpu.CompilerParams(
            collective_id=0, has_side_effects=True, vmem_limit_bytes=56 << 20
        ),
        name="ensemble_gradients",
    )(x[0], grid, edges.T, target.T, area.reshape(1, G), var.reshape(1, VAR), wq, wk, wv, wo, wh.T)
    full = jax.ShapeDtypeStruct((ROWS, D), F32)
    return pl.pallas_call(
        finish_kernel,
        out_shape=(full, full, full, full, jax.ShapeDtypeStruct((ROWS, VAR), F32)),
        in_specs=[vmem, vmem],
        out_specs=(vmem,) * 5,
        name="finish",
    )(rz, wh.T)


def solution(mesh):
    in_specs = (
        P("ens", "space", None),
        P("space", None),
        P("space", None),
        P("space", None),
        P("space"),
        P(),
        P(),
        P(),
        P(),
        P(),
        P(),
    )
    out_specs = (P("space", None),) * 5
    return jax.shard_map(local, mesh=mesh, in_specs=in_specs, out_specs=out_specs, check_vma=False)
```

```python
import functools

import jax
import jax.numpy as jnp
from jax import lax
from jax.experimental import pallas as pl
from jax.experimental.pallas import tpu as pltpu
from jax.sharding import PartitionSpec as P

MESH = pl.DeviceIdType.MESH
HEADS = 16
KNN = 3
FAIR_ALPHA = 0.95
SMOOTH_SQ = 0.0625
ENS = 8
SPACE = 32
CX = 4
CY = 4
CHIPS = CX * CY
D = 1024
HD = D // HEADS
G = 256
M = 64
N = 3 * M
E = KNN * G
VAR = 100
VP = 128
C = D // ENS
ROWS = D // SPACE
W = 256
PAIRS = ENS // 2
BF = jnp.bfloat16
F32 = jnp.float32


def dot(a, b):
    return jnp.dot(a, b, preferred_element_type=F32)


def dot_nt(a, b):
    return lax.dot_general(a, b, (((1,), (1,)), ((), ())), preferred_element_type=F32)


def slope(d):
    return d * lax.rsqrt(d * d + SMOOTH_SQ)


def same_head(width, value):
    rows = lax.broadcasted_iota(jnp.int32, (width, width), 0) // HD
    cols = lax.broadcasted_iota(jnp.int32, (width, width), 1) // HD
    return jnp.where(rows == cols, value, 0.0).astype(BF)


def softmax3(scores):
    s0, s1, s2 = scores[:G], scores[G : 2 * G], scores[2 * G :]
    top = jnp.maximum(jnp.maximum(s0, s1), s2)
    e0, e1, e2 = jnp.exp(s0 - top), jnp.exp(s1 - top), jnp.exp(s2 - top)
    inv = 1.0 / (e0 + e1 + e2)
    return e0 * inv, e1 * inv, e2 * inv


def three(x):
    return jnp.concatenate([x, x, x], axis=0)


def side(x, y):
    return jnp.concatenate([x, y], axis=1)


PLACE = {0: 0, -1: 1, 1: 2, -2: 3, 2: 4, -3: 5, 3: 6, -4: 7, 4: 7}


FAR_FIRST = sorted(range(1, CHIPS), key=lambda t: -min(t // CX, CY - t // CX) - min(t % CX, CX - t % CX))


def main_kernel(
    x_hbm, grid_hbm, edge_ref, target_hbm, area_ref, var_ref,
    wq_hbm, wk_hbm, wv_hbm, wo_hbm, wh_hbm,
    out_hbm,
    grid_ref, target_ref, wh_ref, wq, wk, wv, wo, wht, lat, lat_t, grid_t, mix_t, q, keys, values, attended, hidden,
    delta, wkvc, kg, vg, att_all, att_low, gl, ga, s_v, s_k, oh, oh_t, q3, gq, uct, common, areaw,
    part_ab, part_v, part_qk, sib_ab, sib_v, sib_qk, sum_ab, sum_v, sum_qk, r_ab, r_v, r_qk, rz,
    wsem, ring_s, ring_r, halo_s, halo_l, halo_r, d_s, d_r, sib_s, sib_r, xy_s, xy_r, z_s, z_r, tokens,
):
    e = lax.axis_index("ens")
    s = lax.axis_index("space")
    core = lax.rem(s, 2)
    chip_x = lax.rem(s // 2, CX)
    chip_y = s // (2 * CX)

    def ens_peer(d):
        return (lax.rem(e + d + ENS, ENS), s)

    def space_peer(d):
        return (e, lax.rem(s + d + SPACE, SPACE))

    def chip_peer(t):
        return lax.rem(chip_y + t // CX, CY) * CX + lax.rem(chip_x + lax.rem(t, CX), CX)

    sibling = (e, s + 1 - 2 * core)

    barrier = pltpu.get_barrier_semaphore()

    def greet(peer):
        pl.semaphore_signal(barrier, inc=1, device_id=peer, device_id_type=MESH)

    along_x = [(e, chip_peer(1) * 2 + core), (e, chip_peer(CX - 1) * 2 + core)]
    along_y = [(e, chip_peer(CX) * 2 + core), (e, chip_peer((CY - 1) * CX) * 2 + core)]
    neighbours = [space_peer(1), space_peer(-1), ens_peer(1), ens_peer(-1), *along_x, *along_y]
    for peer in neighbours:
        greet(peer)

    def give_token(i):
        for peer in along_x if i == 0 else along_y:
            pl.semaphore_signal(tokens.at[i], inc=1, device_id=peer, device_id_type=MESH)

    def take_token(i):
        pl.semaphore_wait(tokens.at[i], 2)

    def own_rows(i):
        return pl.ds(i * N + M, M)

    def load(i, src, dst):
        copy = pltpu.make_async_copy(src, dst, wsem.at[i])
        copy.start()
        return copy

    load_x = load(0, x_hbm, lat.at[own_rows(0)])
    load_grid = load(1, grid_hbm, grid_ref)
    load_wq = load(2, wq_hbm, wq)
    loads = [
        load(i + 3, src, dst)
        for i, (src, dst) in enumerate(
            ((wh_hbm, wh_ref), (wk_hbm, wk), (wv_hbm, wv), (wo_hbm, wo), (target_hbm, target_ref))
        )
    ]

    def ring_copy(step, way, half):
        src = pl.ds(PLACE[(1 - step) * way] * N + M + half * (M // 2), M // 2)
        dst = pl.ds(PLACE[-step * way] * N + M + half * (M // 2), M // 2)
        sem = (step - 1) * 4 + (1 - way) + half
        return pltpu.make_async_remote_copy(
            src_ref=lat.at[src], dst_ref=lat.at[dst], send_sem=ring_s.at[sem], recv_sem=ring_r.at[sem],
            device_id=ens_peer(way), device_id_type=MESH,
        )

    ring = {(k, w, h): ring_copy(k, w, h) for k in range(1, 4) for h in (0, 1) for w in (1, -1)}
    ring[4, 1, 0] = ring_copy(4, 1, 0)
    ring[4, -1, 1] = ring_copy(4, -1, 1)

    def pass_on(step, half):
        for way in (1, -1):
            if (step, way, half) in ring:
                ring[step, way, half].wait_recv()
            if (step + 1, way, half) in ring:
                ring[step + 1, way, half].start()

    def halo_copies(i):
        up = pltpu.make_async_remote_copy(
            src_ref=lat.at[own_rows(i)], dst_ref=lat.at[pl.ds(i * N, M)],
            send_sem=halo_s.at[i, 0], recv_sem=halo_l.at[i],
            device_id=space_peer(1), device_id_type=MESH,
        )
        down = pltpu.make_async_remote_copy(
            src_ref=lat.at[own_rows(i)], dst_ref=lat.at[pl.ds(i * N + 2 * M, M)],
            send_sem=halo_s.at[i, 1], recv_sem=halo_r.at[i],
            device_id=space_peer(-1), device_id_type=MESH,
        )
        return up, down

    def start_halo(i):
        for copy in halo_copies(i):
            copy.start()

    def wait_halo(i):
        for copy in halo_copies(i):
            copy.wait_recv()

    load_x.wait()
    pl.semaphore_wait(barrier, len(neighbours))
    start_halo(0)
    for half in (0, 1):
        ring[1, 1, half].start()
        ring[1, -1, half].start()
    give_token(0)

    load_grid.wait()
    load_wq.wait()
    for n in range(D // W):
        cols = slice(n * W, (n + 1) * W)
        q[:, cols] = dot(grid_ref[...], wq[:, cols]).astype(BF)

    for copy in loads:
        copy.wait()
    wht[...] = jnp.zeros_like(wht)
    wht[:VAR, :] = wh_ref[...]
    edges = edge_ref[...]
    slot_rows = (((edges // M) - s + 1 + SPACE) % SPACE) * M + edges % M
    node = lax.broadcasted_iota(jnp.int32, (N, G), 0)
    for j in range(KNN):
        oh_t[:, j * G : (j + 1) * G] = jnp.where(slot_rows[j : j + 1, :] == node, 1.0, 0.0).astype(BF)
    oh[...] = oh_t[...].T
    common[...] = dot_nt(grid_ref[...], wht[...])
    hs = pl.ds(pl.multiple_of(e * C, C), C)
    wkvc[:, :C] = wk[:, hs]
    wkvc[:, C:] = wv[:, hs]
    q3[...] = three(side(q[:, hs], q[:, hs]))

    wait_halo(0)
    pass_on(1, 0)
    take_token(0)
    give_token(1)
    for n in range(D // W):
        cols = slice(n * W, (n + 1) * W)
        keys[:, cols] = dot(lat[:N, :], wk[:, cols]).astype(BF)
        values[:, cols] = dot(lat[:N, :], wv[:, cols]).astype(BF)
        if n == 1:
            pass_on(1, 1)
            start_halo(PLACE[-1])
            start_halo(PLACE[1])

    head_sum = same_head(W, HD**-0.5)
    for n in range(D // W):
        cols = slice(n * W, (n + 1) * W)
        prod = dot(oh[...], keys[:, cols]).astype(BF) * three(q[:, cols])
        att = softmax3(dot(prod, head_sum))
        value_rows = dot(oh[...], values[:, cols])
        total = jnp.zeros((G, W), F32)
        for j in range(KNN):
            total += att[j].astype(BF).astype(F32) * value_rows[j * G : (j + 1) * G]
        attended[:, cols] = total.astype(BF)
        if n == 1:
            pass_on(2, 0)
            take_token(1)
            give_token(2)

    pass_on(2, 1)
    start_halo(PLACE[-2])
    start_halo(PLACE[2])
    for n in range(D // W):
        cols = slice(n * W, (n + 1) * W)
        update = dot(attended[...], wo[:, cols])
        hidden[:, cols] = (grid_ref[:, cols].astype(F32) + update).astype(BF)

    delta[0] = (dot_nt(hidden[...], wht[...]) - common[...]).astype(BF)

    def delta_copy(sem, d_from, d_to, way, rows=slice(None)):
        return pltpu.make_async_remote_copy(
            src_ref=delta.at[PLACE[d_from], rows], dst_ref=delta.at[PLACE[d_to], rows],
            send_sem=d_s.at[sem], recv_sem=d_r.at[sem],
            device_id=ens_peer(way), device_id_type=MESH,
        )

    halves = (pl.ds(0, G // 2), pl.ds(G // 2, G // 2))
    near2 = {(w, h): delta_copy(1 - w + h, 0, -2 * w, 2 * w, halves[h]) for h in (0, 1) for w in (1, -1)}
    near1 = {w: delta_copy(4 + (1 - w) // 2, 0, -w, w) for w in (1, -1)}
    far3 = {(w, h): delta_copy(6 + 1 - w + h, -2 * w, -3 * w, w, halves[h]) for h in (0, 1) for w in (1, -1)}
    far4 = {w: delta_copy(10 + (1 - w) // 2, -2 * w, 4, 2 * w, halves[(1 - w) // 2]) for w in (1, -1)}
    deltas = [*near2.values(), *near1.values(), *far3.values(), *far4.values()]
    for copy in [*near2.values(), *near1.values()]:
        copy.start()

    def pass_delta_on(half):
        for way in (1, -1):
            near2[way, half].wait_recv()
            if half == (1 - way) // 2:
                far4[way].start()
            far3[way, half].start()

    def prepare(p):
        rows = slice(2 * p * N, 2 * (p + 1) * N)
        kv = dot(lat[rows, :], wkvc[...]).astype(BF)
        kg[p] = dot(oh[...], side(kv[:N, :C], kv[N:, :C])).astype(BF)
        vg[p] = dot(oh[...], side(kv[:N, C:], kv[N:, C:])).astype(BF)
        att = softmax3(dot(kg[p] * q3[...], head_sum))
        for j in range(KNN):
            att_all[p, j * G : (j + 1) * G, :] = att[j]
            att_low[p, j * G : (j + 1) * G, :] = att[j].astype(BF)
        lat_t[:, rows] = lat[rows, :].T

    var_row = jnp.concatenate([var_ref[...], jnp.zeros((1, VP - VAR), F32)], axis=1)
    areaw[...] = jnp.broadcast_to(area_ref[...], (VP, G)).T * var_row
    uct[...] = dot_nt(wht[...], wo[hs, :]).astype(BF)
    padded = jnp.concatenate([target_ref[...], jnp.zeros((VP - VAR, G), F32)], axis=0)
    common[...] = common[...] - padded.T
    mix_t[:D, :] = attended[...].T
    pass_on(3, 0)
    wait_halo(1)
    prepare(0)
    pass_on(3, 1)
    start_halo(PLACE[-3])
    start_halo(PLACE[3])
    mix_t[D:, :] = hidden[...].T
    grid_t[...] = grid_ref[...].T
    pass_delta_on(0)
    wait_halo(2)
    wait_halo(3)
    prepare(1)
    pass_delta_on(1)
    pass_on(4, 0)
    pass_on(4, 1)
    start_halo(PLACE[4])
    wait_halo(4)
    wait_halo(5)
    prepare(2)
    fair_eps = (1.0 - FAIR_ALPHA) / ENS
    pair_coef = (1.0 - fair_eps) / (ENS * (ENS - 1))
    step_rows = 16

    def loss_gradient(i):
        rows = pl.ds(pl.multiple_of(i * step_rows, step_rows), step_rows)
        dev = [delta[m, rows, :].astype(F32) for m in range(ENS)]
        pair = [None] * ENS
        for a in range(ENS):
            for b in range(a + 1, ENS):
                t = slope(dev[a] - dev[b])
                pair[a] = t if pair[a] is None else pair[a] + t
                pair[b] = -t if pair[b] is None else pair[b] - t
        shift = common[rows, :]
        scale = areaw[rows, :]
        for m in range(ENS):
            grad = scale * (slope(dev[m] + shift) * (1.0 / ENS) - pair_coef * pair[m])
            gl[pl.ds(pl.multiple_of(m * G + i * step_rows, step_rows), step_rows), :] = grad.astype(BF)

    def loss_gradient_of(half):
        if half == 0:
            near1[1].wait_recv()
            near1[-1].wait_recv()
        far4[1 - 2 * half].wait_recv()
        far3[1, half].wait_recv()
        far3[-1, half].wait_recv()
        steps = G // step_rows // 2
        pl.loop(half * steps, (half + 1) * steps)(loss_gradient)

    loss_gradient_of(0)
    wait_halo(6)
    wait_halo(7)
    prepare(3)
    loss_gradient_of(1)
    take_token(2)

    def sibling_copy(i, part, sib):
        return pltpu.make_async_remote_copy(
            src_ref=part.at[1 - core], dst_ref=sib, send_sem=sib_s.at[i], recv_sem=sib_r.at[i],
            device_id=sibling, device_id_type=MESH,
        )

    def chip_copy(i, summed, r, t):
        chip = chip_peer(t)
        return pltpu.make_async_remote_copy(
            src_ref=summed.at[pl.ds(pl.multiple_of(chip * ROWS, ROWS), ROWS)], dst_ref=r.at[t],
            send_sem=xy_s.at[i, t], recv_sem=xy_r.at[i, t],
            device_id=(e, chip * 2 + core), device_id_type=MESH,
        )

    def spread(i, part, sib, summed, r):
        sibling_copy(i, part, sib).wait_recv()
        summed[...] = (part[core].astype(F32) + sib[...].astype(F32)).astype(BF)

        for t in FAR_FIRST:
            chip_copy(i, summed, r, t).start()

        r[0] = summed[pl.ds(pl.multiple_of((s // 2) * ROWS, ROWS), ROWS), :]

    def last_copy(i, cols, d, m):
        return pltpu.make_async_remote_copy(
            src_ref=rz.at[e, :, cols], dst_ref=rz.at[m, :, cols],
            send_sem=z_s.at[i, d], recv_sem=z_r.at[i, m],
            device_id=ens_peer(d), device_id_type=MESH,
        )

    def collect(i, summed, r, cols):
        @pl.loop(1, CHIPS)
        def _(t):
            chip_copy(i, summed, r, t).wait_recv()

        rz[e, :, cols] = jnp.sum(r[...].astype(F32), axis=0).astype(BF)

        for d in (4, 3, 5, 2, 6, 1, 7):
            last_copy(i, cols, d, e).start()

    def put(part, chunk, cols, value):
        value = value.astype(BF)
        for k in range(W // ROWS):
            dest = chunk * (W // ROWS) + k
            rows = slice((dest // 2) * ROWS, (dest // 2 + 1) * ROWS)
            part[dest % 2, rows, cols] = value[k * ROWS : (k + 1) * ROWS, :]

    ab, v, qk = (0, part_ab, sib_ab), (1, part_v, sib_v), (2, part_qk, sib_qk)
    for i in range(D // W):
        rows = slice(i * W, (i + 1) * W)
        put(part_ab, i, slice(0, VP), dot(mix_t[rows, :], gl[:G, :]))
        put(part_ab, i, slice(VP, 2 * VP), dot(mix_t[D + i * W : D + (i + 1) * W, :], gl[:G, :]))
    sibling_copy(*ab).start()

    for p in range(PAIRS):
        both = dot(gl[p * 2 * G : (p + 1) * 2 * G, :], uct[...]).astype(BF)
        ga[p] = side(both[:G], both[G:])

    def to_nodes(p, sums, s_ref):
        s_ref[2 * p * N : (2 * p + 1) * N, :] = sums[:, :C]
        s_ref[(2 * p + 1) * N : (2 * p + 2) * N, :] = sums[:, C:]

    ones = same_head(W, 1.0)
    for p in range(PAIRS):
        gw = dot(vg[p] * three(ga[p]), ones)
        att = att_all[p]
        t = att * gw
        gs = (att * (gw - three(t[:G] + t[G : 2 * G] + t[2 * G :])) * HD**-0.5).astype(BF)
        gqe = gs.astype(F32) * kg[p].astype(F32)
        gqe = gqe[:G] + gqe[G : 2 * G] + gqe[2 * G :]
        gqe = gqe[:, :C] + gqe[:, C:]
        gq[...] = gqe if p == 0 else gq[...] + gqe
        to_nodes(p, dot(oh_t[...], gs * q3[...]).astype(BF), s_k)
        if p == 1:
            spread(*ab, sum_ab, r_ab)

    for i in range(D // W):
        rows = slice(i * W, (i + 1) * W)
        put(part_qk, i, slice(0, C), dot(grid_t[rows, :], gq[...].astype(BF)))
        put(part_qk, i, slice(C, 2 * C), dot(lat_t[rows, :], s_k[...]))
    sibling_copy(*qk).start()
    for p in range(PAIRS):
        to_nodes(p, dot(oh_t[...], att_low[p] * three(ga[p])).astype(BF), s_v)
    spread(*qk, sum_qk, r_qk)
    for i in range(D // W):
        put(part_v, i, slice(0, C), dot(lat_t[i * W : (i + 1) * W, :], s_v[...]))
    sibling_copy(*v).start()
    qk_cols, v_cols, ab_cols = slice(0, 2 * C), slice(2 * C, 3 * C), slice(3 * C, 3 * C + 2 * VP)
    collect(0, sum_ab, r_ab, ab_cols)
    spread(*v, sum_v, r_v)
    collect(2, sum_qk, r_qk, qk_cols)
    collect(1, sum_v, r_v, v_cols)

    for copy in [*ring.values(), *deltas]:
        copy.wait_send()
    for i in range(ENS):
        for copy in halo_copies(i):
            copy.wait_send()
    stores = []
    for i, summed, r, cols in ((0, sum_ab, r_ab, ab_cols), (2, sum_qk, r_qk, qk_cols), (1, sum_v, r_v, v_cols)):
        sibling_copy(*(ab, v, qk)[i]).wait_send()

        @pl.loop(1, CHIPS)
        def _(t, i=i, summed=summed, r=r):
            chip_copy(i, summed, r, t).wait_send()

        @pl.loop(1, ENS)
        def _(d, i=i, cols=cols):
            last_copy(i, cols, d, e).wait_send()
            last_copy(i, cols, d, lax.rem(e + d, ENS)).wait_recv()

        stores.append(pltpu.make_async_copy(rz.at[:, :, cols], out_hbm.at[:, :, cols], wsem.at[i]))
        stores[-1].start()
    for store in stores:
        store.wait()


def finish_kernel(rz_ref, wh_ref, q_ref, k_ref, v_ref, p_ref, h_ref):
    for m in range(ENS):
        cols = slice(m * C, (m + 1) * C)
        q_ref[:, cols] = rz_ref[m, :, :C].astype(F32)
        k_ref[:, cols] = rz_ref[m, :, C : 2 * C].astype(F32)
        v_ref[:, cols] = rz_ref[m, :, 2 * C : 3 * C].astype(F32)
    mixed = rz_ref[0, :, 3 * C :].astype(F32)
    for m in range(1, ENS):
        mixed += rz_ref[m, :, 3 * C :].astype(F32)
    h_ref[...] = mixed[:, VP : VP + VAR]
    p_ref[...] = dot(mixed[:, :VAR].astype(BF), wh_ref[...])


def local(x, grid, edges, target, area, var, wq, wk, wv, wo, wh):
    vmem = pl.BlockSpec(memory_space=pltpu.VMEM)
    anywhere = pl.BlockSpec(memory_space=pl.ANY)
    dma = pltpu.SemaphoreType.DMA
    widths = (2 * VP, C, 2 * C)
    scratch = [
        pltpu.VMEM((G, D), BF), pltpu.VMEM((VAR, G), F32), pltpu.VMEM((VAR, D), BF),
        *[pltpu.VMEM((D, D), BF)] * 4,
        pltpu.VMEM((VP, D), BF),
        pltpu.VMEM((ENS * N, D), BF), pltpu.VMEM((D, ENS * N), BF),
        pltpu.VMEM((D, G), BF), pltpu.VMEM((2 * D, G), BF),
        pltpu.VMEM((G, D), BF), pltpu.VMEM((N, D), BF), pltpu.VMEM((N, D), BF),
        pltpu.VMEM((G, D), BF), pltpu.VMEM((G, D), BF),
        pltpu.VMEM((ENS, G, VP), BF), pltpu.VMEM((D, 2 * C), BF),
        pltpu.VMEM((PAIRS, E, W), BF), pltpu.VMEM((PAIRS, E, W), BF),
        pltpu.VMEM((PAIRS, E, W), F32), pltpu.VMEM((PAIRS, E, W), BF),
        pltpu.VMEM((ENS * G, VP), BF), pltpu.VMEM((PAIRS, G, W), BF),
        pltpu.VMEM((ENS * N, C), BF), pltpu.VMEM((ENS * N, C), BF),
        pltpu.VMEM((E, N), BF), pltpu.VMEM((N, E), BF),
        pltpu.VMEM((E, W), BF), pltpu.VMEM((G, C), F32), pltpu.VMEM((VP, C), BF),
        pltpu.VMEM((G, VP), F32), pltpu.VMEM((G, VP), F32),
        *[pltpu.VMEM((2, D // 2, w), BF) for w in widths],
        *[pltpu.VMEM((D // 2, w), BF) for w in widths],
        *[pltpu.VMEM((D // 2, w), BF) for w in widths],
        *[pltpu.VMEM((CHIPS, ROWS, w), BF) for w in widths],
        pltpu.VMEM((ENS, ROWS, 3 * C + 2 * VP), BF),
        dma((8,)), dma((16,)), dma((16,)), dma((ENS, 2)), dma((ENS,)), dma((ENS,)),
        dma((12,)), dma((12,)), dma((3,)), dma((3,)), dma((3, CHIPS)), dma((3, CHIPS)),
        dma((3, ENS)), dma((3, ENS)), pltpu.SemaphoreType.REGULAR((3,)),
    ]
    rz = pl.pallas_call(
        main_kernel,
        out_shape=jax.ShapeDtypeStruct((ENS, ROWS, 3 * C + 2 * VP), BF),
        in_specs=[anywhere, anywhere, vmem, anywhere, vmem, vmem] + [anywhere] * 5,
        out_specs=anywhere,
        scratch_shapes=scratch,
        compiler_params=pltpu.CompilerParams(
            collective_id=0, has_side_effects=True, vmem_limit_bytes=56 << 20
        ),
        name="ensemble_gradients",
    )(x[0], grid, edges.T, target.T, area.reshape(1, G), var.reshape(1, VAR), wq, wk, wv, wo, wh.T)
    full = jax.ShapeDtypeStruct((ROWS, D), F32)
    return pl.pallas_call(
        finish_kernel,
        out_shape=(full, full, full, full, jax.ShapeDtypeStruct((ROWS, VAR), F32)),
        in_specs=[vmem, vmem],
        out_specs=(vmem,) * 5,
        name="finish",
    )(rz, wh.T)


def solution(mesh):
    in_specs = (
        P("ens", "space", None),
        P("space", None),
        P("space", None),
        P("space", None),
        P("space"),
        P(),
        P(),
        P(),
        P(),
        P(),
        P(),
    )
    out_specs = (P("space", None),) * 5
    return jax.shard_map(local, mesh=mesh, in_specs=in_specs, out_specs=out_specs, check_vma=False)
```

```python
import functools

import jax
import jax.numpy as jnp
from jax import lax
from jax.experimental import pallas as pl
from jax.experimental.pallas import tpu as pltpu
from jax.sharding import PartitionSpec as P

MESH = pl.DeviceIdType.MESH
HEADS = 16
KNN = 3
FAIR_ALPHA = 0.95
SMOOTH_SQ = 0.0625
ENS = 8
SPACE = 32
CX = 4
CY = 4
CHIPS = CX * CY
D = 1024
HD = D // HEADS
G = 256
M = 64
N = 3 * M
E = KNN * G
VAR = 100
VP = 128
C = D // ENS
ROWS = D // SPACE
W = 256
PAIRS = ENS // 2
BF = jnp.bfloat16
F32 = jnp.float32


def dot(a, b):
    return jnp.dot(a, b, preferred_element_type=F32)


def dot_nt(a, b):
    return lax.dot_general(a, b, (((1,), (1,)), ((), ())), preferred_element_type=F32)


def slope(d):
    return d * lax.rsqrt(d * d + SMOOTH_SQ)


def same_head(width, value):
    rows = lax.broadcasted_iota(jnp.int32, (width, width), 0) // HD
    cols = lax.broadcasted_iota(jnp.int32, (width, width), 1) // HD
    return jnp.where(rows == cols, value, 0.0).astype(BF)


def softmax3(scores):
    s0, s1, s2 = scores[:G], scores[G : 2 * G], scores[2 * G :]
    top = jnp.maximum(jnp.maximum(s0, s1), s2)
    e0, e1, e2 = jnp.exp(s0 - top), jnp.exp(s1 - top), jnp.exp(s2 - top)
    inv = 1.0 / (e0 + e1 + e2)
    return e0 * inv, e1 * inv, e2 * inv


def three(x):
    return jnp.concatenate([x, x, x], axis=0)


def side(x, y):
    return jnp.concatenate([x, y], axis=1)


PLACE = {0: 0, -1: 1, 1: 2, -2: 3, 2: 4, -3: 5, 3: 6, -4: 7, 4: 7}


FAR_FIRST = sorted(range(1, CHIPS), key=lambda t: -min(t // CX, CY - t // CX) - min(t % CX, CX - t % CX))


def main_kernel(
    x_hbm, grid_hbm, edge_ref, target_hbm, area_ref, var_ref,
    wq_hbm, wk_hbm, wv_hbm, wo_hbm, wh_hbm,
    out_hbm,
    grid_ref, target_ref, wh_ref, wq, wk, wv, wo, wht, lat, lat_t, grid_t, mix_t, q, keys, values, attended, hidden,
    delta, wkvc, kg, vg, att_all, att_low, gl, ga, s_v, s_k, oh, oh_t, q3, gq, uct, common, areaw,
    part_ab, part_v, part_qk, sib_ab, sib_v, sib_qk, sum_ab, sum_v, sum_qk, r_ab, r_v, r_qk, rz,
    wsem, ring_s, ring_r, halo_s, halo_l, halo_r, d_s, d_r, sib_s, sib_r, xy_s, xy_r, z_s, z_r, tokens,
):
    e = lax.axis_index("ens")
    s = lax.axis_index("space")
    core = lax.rem(s, 2)
    chip_x = lax.rem(s // 2, CX)
    chip_y = s // (2 * CX)

    def ens_peer(d):
        return (lax.rem(e + d + ENS, ENS), s)

    def space_peer(d):
        return (e, lax.rem(s + d + SPACE, SPACE))

    def chip_peer(t):
        return lax.rem(chip_y + t // CX, CY) * CX + lax.rem(chip_x + lax.rem(t, CX), CX)

    sibling = (e, s + 1 - 2 * core)

    barrier = pltpu.get_barrier_semaphore()

    def greet(peer):
        pl.semaphore_signal(barrier, inc=1, device_id=peer, device_id_type=MESH)

    along_x = [(e, chip_peer(1) * 2 + core), (e, chip_peer(CX - 1) * 2 + core)]
    along_y = [(e, chip_peer(CX) * 2 + core), (e, chip_peer((CY - 1) * CX) * 2 + core)]
    neighbours = [space_peer(1), space_peer(-1), ens_peer(1), ens_peer(-1), *along_x, *along_y]
    for peer in neighbours:
        greet(peer)

    def give_token(i):
        for peer in along_x if i == 0 else along_y:
            pl.semaphore_signal(tokens.at[i], inc=1, device_id=peer, device_id_type=MESH)

    def take_token(i):
        pl.semaphore_wait(tokens.at[i], 2)

    def own_rows(i):
        return pl.ds(i * N + M, M)

    def load(i, src, dst):
        copy = pltpu.make_async_copy(src, dst, wsem.at[i])
        copy.start()
        return copy

    load_x = load(0, x_hbm, lat.at[own_rows(0)])
    load_grid = load(1, grid_hbm, grid_ref)
    load_wq = load(2, wq_hbm, wq)
    loads = [
        load(i + 3, src, dst)
        for i, (src, dst) in enumerate(
            ((wh_hbm, wh_ref), (wk_hbm, wk), (wv_hbm, wv), (wo_hbm, wo), (target_hbm, target_ref))
        )
    ]

    def ring_copy(step, way, half):
        src = pl.ds(PLACE[(1 - step) * way] * N + M + half * (M // 2), M // 2)
        dst = pl.ds(PLACE[-step * way] * N + M + half * (M // 2), M // 2)
        sem = (step - 1) * 4 + (1 - way) + half
        return pltpu.make_async_remote_copy(
            src_ref=lat.at[src], dst_ref=lat.at[dst], send_sem=ring_s.at[sem], recv_sem=ring_r.at[sem],
            device_id=ens_peer(way), device_id_type=MESH,
        )

    ring = {(k, w, h): ring_copy(k, w, h) for k in range(1, 4) for h in (0, 1) for w in (1, -1)}
    ring[4, 1, 0] = ring_copy(4, 1, 0)
    ring[4, -1, 1] = ring_copy(4, -1, 1)

    def pass_on(step, half):
        for way in (1, -1):
            if (step, way, half) in ring:
                ring[step, way, half].wait_recv()
            if (step + 1, way, half) in ring:
                ring[step + 1, way, half].start()

    def halo_copies(i):
        up = pltpu.make_async_remote_copy(
            src_ref=lat.at[own_rows(i)], dst_ref=lat.at[pl.ds(i * N, M)],
            send_sem=halo_s.at[i, 0], recv_sem=halo_l.at[i],
            device_id=space_peer(1), device_id_type=MESH,
        )
        down = pltpu.make_async_remote_copy(
            src_ref=lat.at[own_rows(i)], dst_ref=lat.at[pl.ds(i * N + 2 * M, M)],
            send_sem=halo_s.at[i, 1], recv_sem=halo_r.at[i],
            device_id=space_peer(-1), device_id_type=MESH,
        )
        return up, down

    def start_halo(i):
        for copy in halo_copies(i):
            copy.start()

    def wait_halo(i):
        for copy in halo_copies(i):
            copy.wait_recv()

    load_x.wait()
    pl.semaphore_wait(barrier, len(neighbours))
    start_halo(0)
    for half in (0, 1):
        ring[1, 1, half].start()
        ring[1, -1, half].start()
    give_token(0)

    load_grid.wait()
    load_wq.wait()
    for n in range(D // W):
        cols = slice(n * W, (n + 1) * W)
        q[:, cols] = dot(grid_ref[...], wq[:, cols]).astype(BF)

    for copy in loads:
        copy.wait()
    wht[...] = jnp.zeros_like(wht)
    wht[:VAR, :] = wh_ref[...]
    edges = edge_ref[...]
    slot_rows = (((edges // M) - s + 1 + SPACE) % SPACE) * M + edges % M
    node = lax.broadcasted_iota(jnp.int32, (N, G), 0)
    for j in range(KNN):
        oh_t[:, j * G : (j + 1) * G] = jnp.where(slot_rows[j : j + 1, :] == node, 1.0, 0.0).astype(BF)
    oh[...] = oh_t[...].T
    common[...] = dot_nt(grid_ref[...], wht[...])
    hs = pl.ds(pl.multiple_of(e * C, C), C)
    wkvc[:, :C] = wk[:, hs]
    wkvc[:, C:] = wv[:, hs]
    q3[...] = three(side(q[:, hs], q[:, hs]))

    wait_halo(0)
    pass_on(1, 0)
    take_token(0)
    give_token(1)
    for n in range(D // W):
        cols = slice(n * W, (n + 1) * W)
        keys[:, cols] = dot(lat[:N, :], wk[:, cols]).astype(BF)
        values[:, cols] = dot(lat[:N, :], wv[:, cols]).astype(BF)
        if n == 1:
            pass_on(1, 1)
            start_halo(PLACE[-1])
            start_halo(PLACE[1])

    head_sum = same_head(W, HD**-0.5)
    for n in range(D // W):
        cols = slice(n * W, (n + 1) * W)
        prod = dot(oh[...], keys[:, cols]).astype(BF) * three(q[:, cols])
        att = softmax3(dot(prod, head_sum))
        value_rows = dot(oh[...], values[:, cols])
        total = jnp.zeros((G, W), F32)
        for j in range(KNN):
            total += att[j].astype(BF).astype(F32) * value_rows[j * G : (j + 1) * G]
        attended[:, cols] = total.astype(BF)
        if n == 1:
            pass_on(2, 0)
            take_token(1)
            give_token(2)

    pass_on(2, 1)
    start_halo(PLACE[-2])
    start_halo(PLACE[2])
    for n in range(D // W):
        cols = slice(n * W, (n + 1) * W)
        update = dot(attended[...], wo[:, cols])
        hidden[:, cols] = (grid_ref[:, cols].astype(F32) + update).astype(BF)

    delta[0] = (dot_nt(hidden[...], wht[...]) - common[...]).astype(BF)

    def delta_copy(sem, d_from, d_to, way, rows=slice(None)):
        return pltpu.make_async_remote_copy(
            src_ref=delta.at[PLACE[d_from], rows], dst_ref=delta.at[PLACE[d_to], rows],
            send_sem=d_s.at[sem], recv_sem=d_r.at[sem],
            device_id=ens_peer(way), device_id_type=MESH,
        )

    halves = (pl.ds(0, G // 2), pl.ds(G // 2, G // 2))
    near2 = {(w, h): delta_copy(1 - w + h, 0, -2 * w, 2 * w, halves[h]) for h in (0, 1) for w in (1, -1)}
    near1 = {w: delta_copy(4 + (1 - w) // 2, 0, -w, w) for w in (1, -1)}
    far3 = {(w, h): delta_copy(6 + 1 - w + h, -2 * w, -3 * w, w, halves[h]) for h in (0, 1) for w in (1, -1)}
    far4 = {w: delta_copy(10 + (1 - w) // 2, -2 * w, 4, 2 * w, halves[(1 - w) // 2]) for w in (1, -1)}
    deltas = [*near2.values(), *near1.values(), *far3.values(), *far4.values()]
    for copy in [*near2.values(), *near1.values()]:
        copy.start()

    def pass_delta_on(half):
        for way in (1, -1):
            near2[way, half].wait_recv()
            if half == (1 - way) // 2:
                far4[way].start()
            far3[way, half].start()

    def prepare(p):
        rows = slice(2 * p * N, 2 * (p + 1) * N)
        kv = dot(lat[rows, :], wkvc[...]).astype(BF)
        kg[p] = dot(oh[...], side(kv[:N, :C], kv[N:, :C])).astype(BF)
        vg[p] = dot(oh[...], side(kv[:N, C:], kv[N:, C:])).astype(BF)
        att = softmax3(dot(kg[p] * q3[...], head_sum))
        for j in range(KNN):
            att_all[p, j * G : (j + 1) * G, :] = att[j]
            att_low[p, j * G : (j + 1) * G, :] = att[j].astype(BF)
        lat_t[:, rows] = lat[rows, :].T

    var_row = jnp.concatenate([var_ref[...], jnp.zeros((1, VP - VAR), F32)], axis=1)
    areaw[...] = jnp.broadcast_to(area_ref[...], (VP, G)).T * var_row
    uct[...] = dot_nt(wht[...], wo[hs, :]).astype(BF)
    padded = jnp.concatenate([target_ref[...], jnp.zeros((VP - VAR, G), F32)], axis=0)
    common[...] = common[...] - padded.T
    mix_t[:D, :] = attended[...].T
    pass_on(3, 0)
    wait_halo(1)
    prepare(0)
    pass_on(3, 1)
    start_halo(PLACE[-3])
    start_halo(PLACE[3])
    mix_t[D:, :] = hidden[...].T
    grid_t[...] = grid_ref[...].T
    pass_delta_on(0)
    wait_halo(2)
    wait_halo(3)
    prepare(1)
    pass_delta_on(1)
    pass_on(4, 0)
    pass_on(4, 1)
    start_halo(PLACE[4])
    wait_halo(4)
    wait_halo(5)
    prepare(2)
    fair_eps = (1.0 - FAIR_ALPHA) / ENS
    pair_coef = (1.0 - fair_eps) / (ENS * (ENS - 1))
    step_rows = 16

    def loss_gradient(i):
        rows = pl.ds(pl.multiple_of(i * step_rows, step_rows), step_rows)
        dev = [delta[m, rows, :].astype(F32) for m in range(ENS)]
        pair = [None] * ENS
        for a in range(ENS):
            for b in range(a + 1, ENS):
                t = slope(dev[a] - dev[b])
                pair[a] = t if pair[a] is None else pair[a] + t
                pair[b] = -t if pair[b] is None else pair[b] - t
        shift = common[rows, :]
        scale = areaw[rows, :]
        for m in range(ENS):
            grad = scale * (slope(dev[m] + shift) * (1.0 / ENS) - pair_coef * pair[m])
            gl[pl.ds(pl.multiple_of(m * G + i * step_rows, step_rows), step_rows), :] = grad.astype(BF)

    def loss_gradient_of(half):
        if half == 0:
            near1[1].wait_recv()
            near1[-1].wait_recv()
        far4[1 - 2 * half].wait_recv()
        far3[1, half].wait_recv()
        far3[-1, half].wait_recv()
        steps = G // step_rows // 2
        pl.loop(half * steps, (half + 1) * steps)(loss_gradient)

    loss_gradient_of(0)
    wait_halo(6)
    wait_halo(7)
    prepare(3)
    loss_gradient_of(1)
    take_token(2)

    def sibling_copy(i, part, sib):
        return pltpu.make_async_remote_copy(
            src_ref=part.at[1 - core], dst_ref=sib, send_sem=sib_s.at[i], recv_sem=sib_r.at[i],
            device_id=sibling, device_id_type=MESH,
        )

    def chip_copy(i, summed, r, t):
        chip = chip_peer(t)
        return pltpu.make_async_remote_copy(
            src_ref=summed.at[pl.ds(pl.multiple_of(chip * ROWS, ROWS), ROWS)], dst_ref=r.at[t],
            send_sem=xy_s.at[i, t], recv_sem=xy_r.at[i, t],
            device_id=(e, chip * 2 + core), device_id_type=MESH,
        )

    def spread(i, part, sib, summed, r):
        sibling_copy(i, part, sib).wait_recv()
        summed[...] = (part[core].astype(F32) + sib[...].astype(F32)).astype(BF)

        for t in FAR_FIRST:
            chip_copy(i, summed, r, t).start()

        r[0] = summed[pl.ds(pl.multiple_of((s // 2) * ROWS, ROWS), ROWS), :]

    def last_copy(i, cols, d, m):
        return pltpu.make_async_remote_copy(
            src_ref=rz.at[e, :, cols], dst_ref=rz.at[m, :, cols],
            send_sem=z_s.at[i, d], recv_sem=z_r.at[i, m],
            device_id=ens_peer(d), device_id_type=MESH,
        )

    def collect(i, summed, r, cols):
        @pl.loop(1, CHIPS)
        def _(t):
            chip_copy(i, summed, r, t).wait_recv()

        rz[e, :, cols] = jnp.sum(r[...].astype(F32), axis=0).astype(BF)

        for d in (4, 3, 5, 2, 6, 1, 7):
            last_copy(i, cols, d, e).start()

    def put(part, chunk, cols, value):
        value = value.astype(BF)
        for k in range(W // ROWS):
            dest = chunk * (W // ROWS) + k
            rows = slice((dest // 2) * ROWS, (dest // 2 + 1) * ROWS)
            part[dest % 2, rows, cols] = value[k * ROWS : (k + 1) * ROWS, :]

    ab, v, qk = (0, part_ab, sib_ab), (1, part_v, sib_v), (2, part_qk, sib_qk)
    for i in range(D // W):
        rows = slice(i * W, (i + 1) * W)
        put(part_ab, i, slice(0, VP), dot(mix_t[rows, :], gl[:G, :]))
        put(part_ab, i, slice(VP, 2 * VP), dot(mix_t[D + i * W : D + (i + 1) * W, :], gl[:G, :]))
    sibling_copy(*ab).start()

    for p in range(PAIRS):
        both = dot(gl[p * 2 * G : (p + 1) * 2 * G, :], uct[...]).astype(BF)
        ga[p] = side(both[:G], both[G:])

    def to_nodes(p, sums, s_ref):
        s_ref[2 * p * N : (2 * p + 1) * N, :] = sums[:, :C]
        s_ref[(2 * p + 1) * N : (2 * p + 2) * N, :] = sums[:, C:]

    ones = same_head(W, 1.0)
    for p in range(PAIRS):
        gw = dot(vg[p] * three(ga[p]), ones)
        att = att_all[p]
        t = att * gw
        gs = (att * (gw - three(t[:G] + t[G : 2 * G] + t[2 * G :])) * HD**-0.5).astype(BF)
        gqe = gs.astype(F32) * kg[p].astype(F32)
        gqe = gqe[:G] + gqe[G : 2 * G] + gqe[2 * G :]
        gqe = gqe[:, :C] + gqe[:, C:]
        gq[...] = gqe if p == 0 else gq[...] + gqe
        to_nodes(p, dot(oh_t[...], gs * q3[...]).astype(BF), s_k)
        if p == 1:
            spread(*ab, sum_ab, r_ab)

    for i in range(D // W):
        rows = slice(i * W, (i + 1) * W)
        put(part_qk, i, slice(0, C), dot(grid_t[rows, :], gq[...].astype(BF)))
        put(part_qk, i, slice(C, 2 * C), dot(lat_t[rows, :], s_k[...]))
    sibling_copy(*qk).start()
    for p in range(PAIRS):
        to_nodes(p, dot(oh_t[...], att_low[p] * three(ga[p])).astype(BF), s_v)
    spread(*qk, sum_qk, r_qk)
    for i in range(D // W):
        put(part_v, i, slice(0, C), dot(lat_t[i * W : (i + 1) * W, :], s_v[...]))
    sibling_copy(*v).start()
    qk_cols, v_cols, ab_cols = slice(0, 2 * C), slice(2 * C, 3 * C), slice(3 * C, 3 * C + 2 * VP)
    spread(*v, sum_v, r_v)
    collect(0, sum_ab, r_ab, ab_cols)
    collect(2, sum_qk, r_qk, qk_cols)
    collect(1, sum_v, r_v, v_cols)

    for copy in [*ring.values(), *deltas]:
        copy.wait_send()
    for i in range(ENS):
        for copy in halo_copies(i):
            copy.wait_send()
    stores = []
    for i, summed, r, cols in ((0, sum_ab, r_ab, ab_cols), (2, sum_qk, r_qk, qk_cols), (1, sum_v, r_v, v_cols)):
        sibling_copy(*(ab, v, qk)[i]).wait_send()

        @pl.loop(1, CHIPS)
        def _(t, i=i, summed=summed, r=r):
            chip_copy(i, summed, r, t).wait_send()

        @pl.loop(1, ENS)
        def _(d, i=i, cols=cols):
            last_copy(i, cols, d, e).wait_send()
            last_copy(i, cols, d, lax.rem(e + d, ENS)).wait_recv()

        stores.append(pltpu.make_async_copy(rz.at[:, :, cols], out_hbm.at[:, :, cols], wsem.at[i]))
        stores[-1].start()
    for store in stores:
        store.wait()


def finish_kernel(rz_ref, wh_ref, q_ref, k_ref, v_ref, p_ref, h_ref):
    for m in range(ENS):
        cols = slice(m * C, (m + 1) * C)
        q_ref[:, cols] = rz_ref[m, :, :C].astype(F32)
        k_ref[:, cols] = rz_ref[m, :, C : 2 * C].astype(F32)
        v_ref[:, cols] = rz_ref[m, :, 2 * C : 3 * C].astype(F32)
    mixed = rz_ref[0, :, 3 * C :].astype(F32)
    for m in range(1, ENS):
        mixed += rz_ref[m, :, 3 * C :].astype(F32)
    h_ref[...] = mixed[:, VP : VP + VAR]
    p_ref[...] = dot(mixed[:, :VAR].astype(BF), wh_ref[...])


def local(x, grid, edges, target, area, var, wq, wk, wv, wo, wh):
    vmem = pl.BlockSpec(memory_space=pltpu.VMEM)
    anywhere = pl.BlockSpec(memory_space=pl.ANY)
    dma = pltpu.SemaphoreType.DMA
    widths = (2 * VP, C, 2 * C)
    scratch = [
        pltpu.VMEM((G, D), BF), pltpu.VMEM((VAR, G), F32), pltpu.VMEM((VAR, D), BF),
        *[pltpu.VMEM((D, D), BF)] * 4,
        pltpu.VMEM((VP, D), BF),
        pltpu.VMEM((ENS * N, D), BF), pltpu.VMEM((D, ENS * N), BF),
        pltpu.VMEM((D, G), BF), pltpu.VMEM((2 * D, G), BF),
        pltpu.VMEM((G, D), BF), pltpu.VMEM((N, D), BF), pltpu.VMEM((N, D), BF),
        pltpu.VMEM((G, D), BF), pltpu.VMEM((G, D), BF),
        pltpu.VMEM((ENS, G, VP), BF), pltpu.VMEM((D, 2 * C), BF),
        pltpu.VMEM((PAIRS, E, W), BF), pltpu.VMEM((PAIRS, E, W), BF),
        pltpu.VMEM((PAIRS, E, W), F32), pltpu.VMEM((PAIRS, E, W), BF),
        pltpu.VMEM((ENS * G, VP), BF), pltpu.VMEM((PAIRS, G, W), BF),
        pltpu.VMEM((ENS * N, C), BF), pltpu.VMEM((ENS * N, C), BF),
        pltpu.VMEM((E, N), BF), pltpu.VMEM((N, E), BF),
        pltpu.VMEM((E, W), BF), pltpu.VMEM((G, C), F32), pltpu.VMEM((VP, C), BF),
        pltpu.VMEM((G, VP), F32), pltpu.VMEM((G, VP), F32),
        *[pltpu.VMEM((2, D // 2, w), BF) for w in widths],
        *[pltpu.VMEM((D // 2, w), BF) for w in widths],
        *[pltpu.VMEM((D // 2, w), BF) for w in widths],
        *[pltpu.VMEM((CHIPS, ROWS, w), BF) for w in widths],
        pltpu.VMEM((ENS, ROWS, 3 * C + 2 * VP), BF),
        dma((8,)), dma((16,)), dma((16,)), dma((ENS, 2)), dma((ENS,)), dma((ENS,)),
        dma((12,)), dma((12,)), dma((3,)), dma((3,)), dma((3, CHIPS)), dma((3, CHIPS)),
        dma((3, ENS)), dma((3, ENS)), pltpu.SemaphoreType.REGULAR((3,)),
    ]
    rz = pl.pallas_call(
        main_kernel,
        out_shape=jax.ShapeDtypeStruct((ENS, ROWS, 3 * C + 2 * VP), BF),
        in_specs=[anywhere, anywhere, vmem, anywhere, vmem, vmem] + [anywhere] * 5,
        out_specs=anywhere,
        scratch_shapes=scratch,
        compiler_params=pltpu.CompilerParams(
            collective_id=0, has_side_effects=True, vmem_limit_bytes=56 << 20
        ),
        name="ensemble_gradients",
    )(x[0], grid, edges.T, target.T, area.reshape(1, G), var.reshape(1, VAR), wq, wk, wv, wo, wh.T)
    full = jax.ShapeDtypeStruct((ROWS, D), F32)
    return pl.pallas_call(
        finish_kernel,
        out_shape=(full, full, full, full, jax.ShapeDtypeStruct((ROWS, VAR), F32)),
        in_specs=[vmem, vmem],
        out_specs=(vmem,) * 5,
        name="finish",
    )(rz, wh.T)


def solution(mesh):
    in_specs = (
        P("ens", "space", None),
        P("space", None),
        P("space", None),
        P("space", None),
        P("space"),
        P(),
        P(),
        P(),
        P(),
        P(),
        P(),
    )
    out_specs = (P("space", None),) * 5
    return jax.shard_map(local, mesh=mesh, in_specs=in_specs, out_specs=out_specs, check_vma=False)
```
